128 devices in a mesh: member: 4 (over x), section: 2 (over core), dp: 16 (over z, y).
Axes of the slice: x: 4, y: 4, z: 4, core: 2. Of those that a mesh axis runs over, the one named last changes fastest.
Arguments:
- embeds: bfloat16 [4, 16, 2, 64, 4096], P('member', 'dp'), may hold values from -6 to 6
- lengths: int32 [16, 2], P('dp'), may hold values from 1 to 64, as said below
- route: int32 [16], P('dp'), may hold values from 0 to 15, each once
- w_query: bfloat16 [4, 2, 4096, 2048], P('member', 'section', 'dp'), may hold values from -0.09375 to 0.09375
- w_keyval: bfloat16 [4, 2, 4096, 1024], P('member', 'section', 'dp'), may hold values from -0.09375 to 0.09375
- w_out: bfloat16 [4, 2, 2048, 4096], P('member', 'section', 'dp'), may hold values from -0.125 to 0.125
- norm_gain: float32 [4, 2, 4096], P('member', 'section'), may hold values from 0.5 to 1.5
- head: float32 [4, 4096], P('member'), may hold values from -0.09375 to 0.09375
Outputs:
- scores: float32 [16, 2], P('dp')
- grad_out: float32 [4, 2, 2048, 4096], P('member', 'section', 'dp')
- grad_gain: float32 [4, 2, 4096], P('member', 'section', 'dp')
The draws below stay inside these ranges and needn't reach their ends.
Inputs may be any that keep to these rules, and one draw needn't show every extreme that they name: `lengths`: some sequence fills all 64 positions. `route`: every balanced slot receives exactly one pair.
All inputs are finite; a program needn't handle non-finite values.
Results may differ from the reference program's by a relative error of at most 0.029.
Values may be sent and summed in bfloat16 or wider, within the bound.
A program may use at most 192 MiB of HBM per device.

```python
import jax
import jax.numpy as jnp
from jax import lax

D = 4096
HQ = 16
HK = 4
HS = 128
PAIR_DEV = 1
SEQ = 64
PAIRS = 16
MEMBERS = 4
LAYERS = 2
N_DP = 16


def draw_lengths(key, part):
    key = jax.random.fold_in(key, 7)
    drawn = jax.random.randint(key, (PAIRS, 2), 1, SEQ + 1)
    return drawn.at[0, 0].set(SEQ).astype(jnp.int32)


def block_levels(own_key, extent, shards, least, top_value):
    def one(dim, blocks):
        heights = jax.random.uniform(jax.random.fold_in(jax.random.fold_in(own_key, 6), dim), (blocks,), jnp.float32, least / len(shards), top_value / len(shards))
        return jnp.repeat(jnp.exp(heights), extent[dim] // blocks).reshape((-1,) + (1,) * (len(extent) - dim - 1))

    loudness = one(*shards[0])
    for cut in shards[1:]:
        loudness = loudness * one(*cut)
    return loudness


def gaussian(own_key, dims, scale, most, cuts=(), kind=jnp.bfloat16):
    gain = block_levels(own_key, dims, cuts, -0.22, 0.18) if cuts else 1.0
    result = jax.random.normal(own_key, dims, jnp.float32) * scale * gain
    return jnp.minimum(jnp.maximum(result, -most), most).astype(kind)


def setup_inputs(seed: int = 0) -> dict:
    keys = jax.random.split(jax.random.key(seed), 9)
    return {
        "embeds": gaussian(keys[0], (MEMBERS, PAIRS, 2, SEQ, D), 1.0, 6.0, ((0, 4), (1, 16))),
        "lengths": draw_lengths(jax.random.fold_in(keys[8], 71), 0),
        "route": jax.random.permutation(keys[2], PAIRS).astype(jnp.int32),
        "w_query": gaussian(keys[3], (MEMBERS, LAYERS, D, HQ * HS), D ** -0.5, 0.09375, ((0, 4), (1, 2), (2, 16))),
        "w_keyval": gaussian(keys[4], (MEMBERS, LAYERS, D, 2 * HK * HS), D ** -0.5, 0.09375, ((0, 4), (1, 2), (2, 16))),
        "w_out": gaussian(keys[5], (MEMBERS, LAYERS, HQ * HS, D), (HQ * HS) ** -0.5, 0.125, ((0, 4), (1, 2), (2, 16))),
        "norm_gain": jnp.clip(1.0 + 0.1 * jax.random.normal(keys[6], (MEMBERS, LAYERS, D), jnp.float32), 0.5, 1.5),
        "head": gaussian(keys[7], (MEMBERS, D), D ** -0.5, 0.09375, ((0, 4),), jnp.float32),
    }


EPS = 1e-05

def unit_rows(widened):
    return widened * lax.rsqrt(lax.optimization_barrier(jnp.mean(widened * widened, -1, keepdims=True)) + EPS)

def rms_scale(widened, norm_scale):
    return unit_rows(widened) * norm_scale

def attend(queries, keyvals):
    seq_count, positions, feat_width = queries.shape
    head_count = feat_width // HS
    shared_heads = keyvals.shape[-1] // (2 * HS)
    group_size = head_count // shared_heads
    query_heads = queries.reshape(seq_count, positions, shared_heads, group_size, HS)
    key_rows = keyvals[..., :shared_heads * HS].reshape(seq_count, positions, shared_heads, HS)
    value_rows = keyvals[..., shared_heads * HS:].reshape(seq_count, positions, shared_heads, HS)
    logits = jnp.einsum('nqhgd,nkhd->nhgqk', query_heads, key_rows, precision=lax.Precision.HIGHEST) * HS ** (-0.5)
    causal = jnp.arange(positions)[:, None] >= jnp.arange(positions)[None, :]
    weights = jnp.where(causal, jnp.exp(jnp.where(causal, logits, 0.0)), 0.0)
    weights = weights / lax.optimization_barrier(jnp.sum(weights, -1, keepdims=True))
    weights = lax.optimization_barrier(weights.astype(jnp.bfloat16)).astype(jnp.float32)
    context = jnp.einsum('nhgqk,nkhd->nqhgd', weights, value_rows, precision=lax.Precision.HIGHEST)
    return context.reshape(seq_count, positions, feat_width)

def segment_forward(hidden, norm_scale, query_proj, keyval_proj, out_proj):
    seq_count, positions, model_width = hidden.shape
    widened = hidden.astype(jnp.float32)
    normed = rms_scale(widened, norm_scale).astype(jnp.bfloat16).reshape(seq_count * positions, model_width)
    queries = jnp.dot(normed, query_proj, preferred_element_type=jnp.float32).astype(jnp.bfloat16)
    keyvals = jnp.dot(normed, keyval_proj, preferred_element_type=jnp.float32).astype(jnp.bfloat16)
    context = attend(queries.reshape(seq_count, positions, -1).astype(jnp.float32), keyvals.reshape(seq_count, positions, -1).astype(jnp.float32))
    context = context.astype(jnp.bfloat16).reshape(seq_count * positions, -1)
    update = jnp.dot(context, out_proj, preferred_element_type=jnp.float32)
    output = (widened + update.reshape(seq_count, positions, model_width)).astype(jnp.bfloat16)
    return (output, (hidden, queries, keyvals, context))

def branch_back(grad_now, residuals, norm_scale, query_proj, keyval_proj, out_proj):
    hidden, queries, keyvals, context = residuals
    seq_count, positions, model_width = hidden.shape
    row_count = seq_count * positions
    grad_rows = grad_now.reshape(row_count, model_width)
    grad_context = lax.dot_general(grad_rows, out_proj, (((1,), (1,)), ((), ())), preferred_element_type=jnp.float32)
    _, pull_attend = jax.vjp(attend, queries.reshape(seq_count, positions, -1).astype(jnp.float32), keyvals.reshape(seq_count, positions, -1).astype(jnp.float32))
    grad_query, grad_keyval = pull_attend(grad_context.reshape(seq_count, positions, -1))
    grad_normed = lax.dot_general(grad_query.astype(jnp.bfloat16).reshape(row_count, -1), query_proj, (((1,), (1,)), ((), ())), preferred_element_type=jnp.float32)
    grad_normed = grad_normed + lax.dot_general(grad_keyval.astype(jnp.bfloat16).reshape(row_count, -1), keyval_proj, (((1,), (1,)), ((), ())), preferred_element_type=jnp.float32)
    widened = hidden.astype(jnp.float32)
    _, pull_norm = jax.vjp(lambda rows_in: rms_scale(rows_in, norm_scale), widened)
    grad_hidden, = pull_norm(grad_normed.reshape(seq_count, positions, model_width))
    new_grad = (grad_now.astype(jnp.float32) + grad_hidden).astype(jnp.bfloat16)
    return (new_grad, grad_normed)

def pick_last(final, seq_lens):
    last_mask = jnp.arange(final.shape[1])[None, :] == (seq_lens - 1)[:, None]
    picked = lax.optimization_barrier(jnp.sum(jnp.where(last_mask[:, :, None], final.astype(jnp.float32), 0.0), axis=1))
    return (picked, last_mask)

def score_of(last_rows, head_vec):
    return lax.optimization_barrier(jnp.sum(rms_scale(last_rows, head_vec), -1))

def seed_of(final, seq_lens, head_vec, ensemble):
    last_rows, last_mask = pick_last(final, seq_lens)
    spread = jax.nn.sigmoid(ensemble[:, 1] - ensemble[:, 0])
    direction = jnp.stack([-spread, spread], -1).reshape(-1)
    _, pull_score = jax.vjp(lambda rows_in: score_of(rows_in, head_vec), last_rows)
    grad_last, = pull_score(direction)
    return jnp.where(last_mask[:, :, None], grad_last[:, None, :], 0.0).astype(jnp.bfloat16)

def reference(embeds, lengths, route, w_query, w_keyval, w_out, norm_gain, head):
    members = embeds.shape[0]
    layers = w_query.shape[1]
    balanced = jnp.zeros_like(embeds).at[:, route].set(embeds)
    seq_lens = jnp.zeros_like(lengths).at[route].set(lengths).reshape(-1)
    sequences = balanced.reshape(members, PAIRS * 2, SEQ, D)
    rows_group = 2 * PAIR_DEV * SEQ

    def run_forward(hidden, query_all, keyval_all, out_all, gain_all):
        stored = []
        for layer in range(layers):
            hidden, residuals = segment_forward(hidden, gain_all[layer], query_all[layer], keyval_all[layer], out_all[layer])
            stored.append(residuals)
        return (hidden, stored)

    def member_score(operands):
        hidden, query_all, keyval_all, out_all, gain_all, head_vec = operands
        final, _ = run_forward(hidden, query_all, keyval_all, out_all, gain_all)
        return score_of(pick_last(final, seq_lens)[0], head_vec)
    member_scores = lax.map(member_score, (sequences, w_query, w_keyval, w_out, norm_gain, head))
    ensemble = (lax.optimization_barrier(jnp.sum(member_scores, 0)) / members).reshape(PAIRS, 2)

    def member_grads(operands):
        hidden, query_all, keyval_all, out_all, gain_all, head_vec = operands
        final, stored = run_forward(hidden, query_all, keyval_all, out_all, gain_all)
        grad_now = seed_of(final, seq_lens, head_vec, ensemble)
        out_terms = [None] * layers
        gain_terms = [None] * layers
        for layer in reversed(range(layers)):
            residuals = stored[layer]
            new_grad, grad_normed = branch_back(grad_now, residuals, gain_all[layer], query_all[layer], keyval_all[layer], out_all[layer])
            grad_rows = grad_now.reshape(N_DP, rows_group, D).astype(jnp.float32)
            context_rows = residuals[3].reshape(N_DP, rows_group, -1).astype(jnp.float32)
            partial_out = jnp.einsum('grc,grd->gcd', context_rows, grad_rows)
            out_terms[layer] = lax.optimization_barrier(jnp.sum(lax.optimization_barrier(partial_out.astype(jnp.bfloat16)).astype(jnp.float32), 0))
            unit_part = unit_rows(residuals[0].astype(jnp.float32)).reshape(N_DP, rows_group, D)
            gain_part = lax.optimization_barrier(jnp.sum(grad_normed.reshape(N_DP, rows_group, D) * unit_part, 1))
            gain_terms[layer] = lax.optimization_barrier(jnp.sum(lax.optimization_barrier(gain_part.astype(jnp.bfloat16)).astype(jnp.float32), 0))
            grad_now = new_grad
        return (jnp.stack(out_terms), jnp.stack(gain_terms))
    grad_out, grad_gain = lax.map(member_grads, (sequences, w_query, w_keyval, w_out, norm_gain, head))
    return (ensemble, grad_out, grad_gain)
```

```python
import jax
import jax.numpy as jnp
from jax import lax
from jax.experimental import pallas as pl
from jax.experimental.pallas import tpu as pltpu
from jax.sharding import PartitionSpec as P

MESH = pl.DeviceIdType.MESH
F32 = jnp.float32
BF16 = jnp.bfloat16
EPS = 1e-05
HS = 128
SEQ = 64
D = 4096
RING = 4
N_DP = RING * RING
HEADS = 16
GROUP = HEADS // RING
QW = GROUP * HS
ROWS = RING * SEQ
BLK = D // N_DP
HALF = D // 2
SCALE = HS ** (-0.5)
N_SEMS = 112


def mm(a, b):
    return jnp.dot(a, b, preferred_element_type=F32)


def nt(a, b):
    return lax.dot_general(a, b, (((1,), (1,)), ((), ())), preferred_element_type=F32)


def tn(a, b):
    return lax.dot_general(a, b, (((0,), (0,)), ((), ())), preferred_element_type=F32)


def kernel(
    emb, lens, route, wq, wkv, wo, gain, head,
    scores_out, grad_out, gain_out,
    X, GA, HD, N, WQ, WKV, WO, WQ1, WO1, WKV1,
    QA, KVA, QB, KVB, WA, CTX, CTT, CTP, OP, FWD, LAND,
    H1, N1, KVA1, KC, VC, Q16,
    NL, HL, S1, R1, X1, T2, R2, S3, R3, X3, T4, R4, SCB, S6, R6, X6, T7, R7, DC,
    S8, R8, X8, T9, R9, GNL, XC, GC, GN, DKV,
    G, GP, DCT, DQB, DKVB, GOP, FWD2, LAND2, SG, RG, SP, PG,
    ssem, rsem, lsem,
):
    s = lax.axis_index("section")
    m = lax.axis_index("member")
    dp = lax.axis_index("dp")
    z = dp // RING
    y = dp % RING
    other = 1 - s
    zr, zl, zo = (z + 1) % RING, (z + 3) % RING, (z + 2) % RING
    yr, yl, yo = (y + 1) % RING, (y + 3) % RING, (y + 2) % RING
    at_zr, at_zl, at_zo = zr * RING + y, zl * RING + y, zo * RING + y
    at_yr, at_yl = z * RING + yr, z * RING + yl
    is0 = s == 0
    is1 = s == 1
    ids = {}
    pending = []

    def desc(name, src, dst, **dev):
        i = ids.setdefault(name, len(ids))
        return pltpu.make_async_remote_copy(
            src_ref=src, dst_ref=dst, send_sem=ssem.at[i], recv_sem=rsem.at[i],
            device_id=dev, device_id_type=MESH,
        )

    def guarded(cond, act):
        if cond is None:
            act()
        else:
            pl.when(cond)(act)

    def send(cond, *items):
        copies = [desc(name, src, dst, **dev) for name, src, dst, dev in items]

        def act():
            for c in copies:
                c.start()

        guarded(cond, act)

        def fin():
            for c in copies:
                c.wait_send()

        pending.append((cond, fin))

    def recv(cond, *items):
        copies = [desc(name, dst, dst, section=other) for name, dst in items]

        def act():
            for c in copies:
                c.wait_recv()

        guarded(cond, act)

    def exchange(name, src_of, land):
        i = ids.setdefault(name, len(ids))

        @pl.loop(1, N_DP)
        def _(k):
            peer = (dp + k) % N_DP
            pltpu.make_async_remote_copy(
                src_ref=src_of(peer, N_DP - 1 - k), dst_ref=land.at[k - 1],
                send_sem=ssem.at[i], recv_sem=rsem.at[i],
                device_id={"dp": peer}, device_id_type=MESH,
            ).start()

        whole = desc(name, land.at[pl.ds(0, N_DP - 1)], land.at[pl.ds(0, N_DP - 1)], section=other)
        pending.append((None, whole.wait_send))

    def landed(name, land):
        desc(name, land.at[pl.ds(0, N_DP - 1)], land.at[pl.ds(0, N_DP - 1)], section=other).wait_recv()

    def slot_of(h):
        return (dp + N_DP - 1 - h) % N_DP

    lx = pltpu.make_async_copy(emb.at[0, 0, s], X, lsem.at[0])
    lg = pltpu.make_async_copy(gain.at[0], GA.at[s], lsem.at[1])
    lh = pltpu.make_async_copy(head, HD, lsem.at[2])
    lx.start()
    lg.start()
    lh.start()
    wq_mine, wkv_mine, wo_mine = wq.at[0, 0], wkv.at[0, 0], wo.at[0, 0]

    def cols(ref, first, size):
        return ref.at[:, pl.ds(pl.multiple_of(first, HS), size)]

    def slices(dest_z):
        return (
            (cols(wq_mine, dest_z * QW, QW), WQ.at[y, z]),
            (cols(wkv_mine, dest_z * HS, HS), WKV.at[y, z, :, pl.ds(0, HS)]),
            (cols(wkv_mine, RING * HS + dest_z * HS, HS), WKV.at[y, z, :, pl.ds(HS, HS)]),
        )

    wo_rows = lambda yy: WO.at[pl.ds(pl.multiple_of(yy * HS, HS), HS)]
    local0 = [pltpu.make_async_copy(a, b, lsem.at[3 + n]) for n, (a, b) in enumerate(slices(z))]
    local0.append(pltpu.make_async_copy(wo_mine, wo_rows(y), lsem.at[6]))
    local1 = [
        pltpu.make_async_copy(wq_mine, WQ1, lsem.at[3]),
        pltpu.make_async_copy(wkv_mine, WKV1.at[y, z], lsem.at[4]),
        pltpu.make_async_copy(wo_mine, WO1, lsem.at[5]),
    ]

    @pl.when(is0)
    def _():
        for c in local0:
            c.start()

    @pl.when(is1)
    def _():
        for c in local1:
            c.start()

    barrier = pltpu.get_barrier_semaphore()

    @pl.loop(1, N_DP)
    def _(k):
        pl.semaphore_signal(barrier, inc=1, device_id={"dp": (dp + k) % N_DP}, device_id_type=MESH)

    for dm in range(4):
        for ds in range(2):
            if dm or ds:
                pl.semaphore_signal(
                    barrier, inc=1, device_id={"member": (m + dm) % 4, "section": (s + ds) % 2},
                    device_id_type=MESH,
                )
    for at in (at_yr, at_yl):
        pl.semaphore_signal(barrier, inc=1, device_id={"section": other, "dp": at}, device_id_type=MESH)
    pl.semaphore_wait(barrier, N_DP - 1 + 7 + 2)

    for far, at in ((1, at_zr), (3, at_zl), (2, at_zo)):
        dest = (z + far) % RING
        send(is0, *[(f"a2a{far}{n}", a, b, {"dp": at}) for n, (a, b) in enumerate(slices(dest))])
    mine = wo_rows(y)
    send(is0,
         ("wo_r", wo_mine, mine, {"dp": at_yr}),
         ("wo_l", wo_mine, mine, {"dp": at_yl}),
         ("wo_c", wo_mine, mine, {"section": 1}))
    send(None, ("gain", gain.at[0], GA.at[s], {"section": other}))

    lx.wait()
    lg.wait()
    lh.wait()
    recv(None, ("gain", GA.at[other]))
    my_rows = lambda zz: pl.ds(pl.multiple_of(zz * SEQ, SEQ), SEQ)

    @pl.loop(0, 4)
    def _(g):
        part = pl.ds(pl.multiple_of(g * 16, 16), 16)
        rows = X[part, :].astype(F32)
        unit = rows * lax.rsqrt(jnp.mean(rows * rows, -1, keepdims=True) + EPS)
        N[pl.ds(pl.multiple_of(z * SEQ + g * 16, 16), 16), :] = (unit * GA[0]).astype(BF16)

    def half_rows(ref, zz, half):
        return ref.at[pl.ds(pl.multiple_of(zz * SEQ + half * 32, 32), 32)]

    def ring_z1(name, ref):
        block = ref.at[my_rows(z)]
        send(None, (name + "r", block, block, {"dp": at_zr}), (name + "l", block, block, {"dp": at_zl}))

    def ring_z2(name, ref):
        recv(None, (name + "r", ref.at[my_rows(zl)]))
        a = half_rows(ref, zl, 0)
        send(None, (name + "R", a, a, {"dp": at_zr}))
        recv(None, (name + "l", ref.at[my_rows(zr)]))
        b = half_rows(ref, zr, 1)
        send(None, (name + "L", b, b, {"dp": at_zl}))

    def ring_z3(name, ref):
        recv(None, (name + "R", half_rows(ref, zo, 0)), (name + "L", half_rows(ref, zo, 1)))

    ring_z1("n", N)

    @pl.when(is0)
    def _():
        for c in local0:
            c.wait()

    for far, zz in ((1, zl), (3, zr), (2, zo)):
        recv(is0, (f"a2a{far}0", WQ.at[y, zz]),
             (f"a2a{far}1", WKV.at[y, zz, :, pl.ds(0, HS)]),
             (f"a2a{far}2", WKV.at[y, zz, :, pl.ds(HS, HS)]))
    send(is0,
         ("wq_r", WQ.at[y], WQ.at[y], {"dp": at_yr}),
         ("wq_l", WQ.at[y], WQ.at[y], {"dp": at_yl}),
         ("wk_r", WKV.at[y], WKV.at[y], {"dp": at_yr}),
         ("wk_l", WKV.at[y], WKV.at[y], {"dp": at_yl}),
         ("wq_c", WQ.at[y], WQ.at[y], {"section": 1}),
         ("wk_c", WKV.at[y], WKV.at[y], {"section": 1}))

    @pl.when(is1)
    def _():
        for c in local1:
            c.wait()

    kv_mine = WKV1.at[y, z]
    send(is1,
         ("q1", WQ1, WQ1, {"section": 0}),
         ("o1", WO1, WO1, {"section": 0}))
    ring_z2("n", N)
    send(is1,
         ("k1r", kv_mine, kv_mine, {"dp": at_zr}),
         ("k1l", kv_mine, kv_mine, {"dp": at_zl}))

    def wo_half(yy, half):
        return WO.at[pl.ds(pl.multiple_of(yy * HS + half * 64, 64), 64)]

    def two(ref, yy, half):
        return ref.at[yy, pl.ds(2 * half, 2)]

    recv(is0, ("wo_r", wo_rows(yl)))
    send(is0, ("wo_R", wo_half(yl, 0), wo_half(yl, 0), {"dp": at_yr}),
         ("wo_cl", wo_rows(yl), wo_rows(yl), {"section": 1}))
    recv(is0, ("wo_l", wo_rows(yr)))
    send(is0, ("wo_L", wo_half(yr, 1), wo_half(yr, 1), {"dp": at_yl}),
         ("wo_cr", wo_rows(yr), wo_rows(yr), {"section": 1}))
    k1_half = lambda yy, zz, half: WKV1.at[yy, zz, pl.ds(half * 128, 128)]
    recv(is1, ("k1r", WKV1.at[y, zl]))
    send(is1, ("k1R", k1_half(y, zl, 0), k1_half(y, zl, 0), {"dp": at_zr}))
    recv(is1, ("k1l", WKV1.at[y, zr]))
    send(is1, ("k1L", k1_half(y, zr, 1), k1_half(y, zr, 1), {"dp": at_zl}))

    QA[...] = jnp.zeros_like(QA)
    KVA[...] = jnp.zeros_like(KVA)

    def project(yy):
        @pl.loop(0, RING)
        def _(zz):
            block = N[:, pl.ds(pl.multiple_of((zz * RING + yy) * BLK, BLK), BLK)]
            QA[...] += mm(block, WQ[yy, zz])
            KVA[...] += mm(block, WKV[yy, zz])

    ring_z3("n", N)
    recv(is1, ("wq_c", WQ.at[y]), ("wk_c", WKV.at[y]))
    project(y)
    for tag, yy, fwd, half, at, back in (("r", yl, "R", 0, at_yr, "cl"), ("l", yr, "L", 1, at_yl, "cr")):
        recv(is0, ("wq_" + tag, WQ.at[yy]), ("wk_" + tag, WKV.at[yy]))
        send(is0,
             ("wq_" + fwd, two(WQ, yy, half), two(WQ, yy, half), {"dp": at}),
             ("wk_" + fwd, two(WKV, yy, half), two(WKV, yy, half), {"dp": at}),
             ("wq_" + back, WQ.at[yy], WQ.at[yy], {"section": 1}),
             ("wk_" + back, WKV.at[yy], WKV.at[yy], {"section": 1}))
    for back, yy in (("cl", yl), ("cr", yr)):
        recv(is1, ("wq_" + back, WQ.at[yy]), ("wk_" + back, WKV.at[yy]))
        project(yy)
    recv(is0, ("wo_R", wo_half(yo, 0)), ("wo_L", wo_half(yo, 1)))
    send(is0, ("wo_co", wo_rows(yo), wo_rows(yo), {"section": 1}))
    recv(is0, ("wq_R", two(WQ, yo, 0)), ("wk_R", two(WKV, yo, 0)),
         ("wq_L", two(WQ, yo, 1)), ("wk_L", two(WKV, yo, 1)))
    send(is0, ("wq_co", WQ.at[yo], WQ.at[yo], {"section": 1}),
         ("wk_co", WKV.at[yo], WKV.at[yo], {"section": 1}))
    recv(is1, ("wq_co", WQ.at[yo]), ("wk_co", WKV.at[yo]))
    recv(is1, ("k1R", k1_half(y, zo, 0)), ("k1L", k1_half(y, zo, 1)))
    send(is1,
         ("k1yr", WKV1.at[y], WKV1.at[y], {"dp": at_yr}),
         ("k1yl", WKV1.at[y], WKV1.at[y], {"dp": at_yl}),
         ("k1c", WKV1.at[y], WKV1.at[y], {"section": 0}))
    project(yo)
    QB[...] = QA[...].astype(BF16)
    KVB[...] = KVA[...].astype(BF16)

    r_i = lax.broadcasted_iota(jnp.int32, (ROWS, ROWS), 0)
    c_i = lax.broadcasted_iota(jnp.int32, (ROWS, ROWS), 1)
    seen = jnp.logical_and(r_i // SEQ == c_i // SEQ, c_i <= r_i)
    for h in range(GROUP):
        span = slice(h * HS, (h + 1) * HS)
        logits = nt(QB[:, span], KVB[:, :HS]) * SCALE
        grown = jnp.where(seen, jnp.exp(jnp.where(seen, logits, 0.0)), 0.0)
        weights = grown / jnp.sum(grown, -1, keepdims=True)
        WA[h] = weights
        context = mm(weights.astype(BF16), KVB[:, HS:])
        CTX[:, span] = context.astype(BF16)
        CTT[span, :] = context.T.astype(BF16)
    send(None, ("ctt", CTT, CTP, {"section": other}))

    recv(is1, ("wo_c", wo_rows(y)), ("wo_cl", wo_rows(yl)), ("wo_cr", wo_rows(yr)), ("wo_co", wo_rows(yo)))

    @pl.loop(0, 8)
    def _(t):
        span = pl.ds(pl.multiple_of(t * 512, 512), 512)
        OP[:, span] = mm(CTX[...], WO[:, span]).astype(BF16)

    send(None, ("o1r", half_rows(OP, zo, 0), FWD.at[0], {"dp": at_zr}),
         ("o1l", half_rows(OP, zo, 1), FWD.at[1], {"dp": at_zl}))
    for side, tag, dest, at in ((0, "o1r", zr, at_zr), (1, "o1l", zl, at_zl)):
        recv(None, (tag, FWD.at[side]))

        @pl.loop(0, 2)
        def _(g):
            rows = pl.ds(pl.multiple_of(dest * SEQ + side * 32 + g * 16, 16), 16)
            part = pl.ds(pl.multiple_of(g * 16, 16), 16)
            OP[rows, :] = (OP[rows, :].astype(F32) + FWD[side, part, :].astype(F32)).astype(BF16)

        send(None, (f"o2{side}", OP.at[my_rows(dest)], LAND.at[side], {"dp": at}))

    for tag, yy, fwd, half, at in (("r", yl, "R", 0, at_yr), ("l", yr, "L", 1, at_yl)):
        recv(is1, ("k1y" + tag, WKV1.at[yy]))
        send(is1, ("k1y" + fwd, two(WKV1, yy, half), two(WKV1, yy, half), {"dp": at}),
             ("k1c" + tag, WKV1.at[yy], WKV1.at[yy], {"section": 0}))

    recv(None, ("o20", LAND.at[0]), ("o21", LAND.at[1]))

    length = jnp.where(is0, lens[0, 0], lens[0, 1])
    NL[...] = jnp.zeros_like(NL)
    HL[...] = jnp.zeros_like(HL)

    def last_rows(g):
        return lax.broadcasted_iota(jnp.int32, (16, D), 0) + g * 16 == length - 1

    @pl.loop(0, 4)
    def _(g):
        part = pl.ds(pl.multiple_of(g * 16, 16), 16)
        own = pl.ds(pl.multiple_of(z * SEQ + g * 16, 16), 16)
        total = X[part, :].astype(F32) + (
            OP[own, :].astype(F32) + LAND[0, part, :].astype(F32) + LAND[1, part, :].astype(F32)
        )
        hidden = total.astype(BF16)
        H1[part, :] = hidden
        rows = hidden.astype(F32)
        unit = rows * lax.rsqrt(jnp.mean(rows * rows, -1, keepdims=True) + EPS)
        normed = (unit * GA[1]).astype(BF16)
        N1[part, :] = normed
        last = last_rows(g)
        NL[...] += jnp.sum(jnp.where(last, normed.astype(F32), 0.0), 0, keepdims=True)
        HL[...] += jnp.sum(jnp.where(last, rows, 0.0), 0, keepdims=True)

    for j in range(N_DP):
        S1[j] = NL[:, j * BLK : (j + 1) * BLK]
    exchange("e1", lambda peer, slot: S1.at[peer], R1)
    R1[N_DP - 1] = S1[dp]
    KVA1[...] = jnp.zeros_like(KVA1)

    def project1(yy):
        @pl.loop(0, RING)
        def _(zz):
            block = N1[:, pl.ds(pl.multiple_of((zz * RING + yy) * BLK, BLK), BLK)]
            KVA1[...] += mm(block, WKV1[yy, zz])

    recv(is0, ("q1", WQ1), ("o1", WO1), ("k1c", WKV1.at[y]))
    project1(y)
    landed("e1", R1)
    for j in range(N_DP):
        X1[j : j + 1, :] = R1[j]
    back = mm(X1[...].astype(BF16), WQ1[...])
    for j in range(N_DP):
        T2[j] = back[j : j + 1, :]
    exchange("e2", lambda peer, slot: T2.at[slot], R2)
    R2[N_DP - 1] = T2[N_DP - 1]
    for tag, yy in (("r", yl), ("l", yr)):
        recv(is0, ("k1c" + tag, WKV1.at[yy]))
        project1(yy)
    recv(is1, ("k1yR", two(WKV1, yo, 0)), ("k1yL", two(WKV1, yo, 1)))
    send(is1, ("k1co", WKV1.at[yo], WKV1.at[yo], {"section": 0}))
    recv(is0, ("k1co", WKV1.at[yo]))
    project1(yo)
    for g in range(RING):
        KC[g * SEQ : (g + 1) * SEQ, :] = KVA1[:, g * HS : (g + 1) * HS].astype(BF16)
        VC[g * SEQ : (g + 1) * SEQ, :] = KVA1[:, (RING + g) * HS : (RING + g + 1) * HS].astype(BF16)
    landed("e2", R2)
    q_row = R2[0]
    for j in range(1, N_DP):
        q_row = q_row + R2[j]
    for h in range(HEADS):
        Q16[h : h + 1, :] = q_row[:, h * HS : (h + 1) * HS]
    q_last = Q16[...].astype(BF16)

    h_i = lax.broadcasted_iota(jnp.int32, (HEADS, RING * SEQ), 0)
    k_i = lax.broadcasted_iota(jnp.int32, (HEADS, RING * SEQ), 1)
    seen1 = jnp.logical_and(h_i // GROUP == k_i // SEQ, k_i % SEQ < length)
    logits = nt(q_last, KC[...]) * SCALE
    grown = jnp.where(seen1, jnp.exp(jnp.where(seen1, logits, 0.0)), 0.0)
    weights1 = grown / jnp.sum(grown, -1, keepdims=True)
    probs1 = weights1.astype(BF16)
    context1 = mm(probs1, VC[...]).astype(BF16).astype(F32)
    for h in range(HEADS):
        S3[h] = context1[h : h + 1, :]
    exchange("e3", lambda peer, slot: S3.at[peer], R3)
    R3[N_DP - 1] = S3[dp]
    landed("e3", R3)
    for j in range(N_DP):
        X3[j : j + 1, :] = R3[j]
    x3 = X3[...].astype(BF16)
    for t in range(4):
        back = mm(x3, WO1[:, t * 1024 : (t + 1) * 1024])
        for j in range(N_DP):
            T4[j, :, t * 1024 : (t + 1) * 1024] = back[j : j + 1, :]
    exchange("e4", lambda peer, slot: T4.at[slot], R4)
    R4[N_DP - 1] = T4[N_DP - 1]
    landed("e4", R4)
    update = R4[0]
    for j in range(1, N_DP):
        update = update + R4[j]
    final = (HL[...] + update).astype(BF16).astype(F32)

    scale1 = lax.rsqrt(jnp.mean(final * final, -1, keepdims=True) + EPS)
    unit1 = final * scale1
    weighed = unit1 * HD[...]
    score = jnp.sum(weighed, -1, keepdims=True)
    mine_sc = m * 2 + s
    SCB[mine_sc] = jnp.broadcast_to(score, (1, HS))
    send(None, *[
        (f"sc{dm}{ds}", SCB.at[mine_sc], SCB.at[mine_sc], {"member": (m + dm) % 4, "section": (s + ds) % 2})
        for dm in range(4) for ds in range(2) if dm or ds
    ])
    toward = scale1 * (HD[...] - unit1 * (score / D))
    S6[...] = toward.astype(BF16).astype(F32)
    exchange("e6", lambda peer, slot: S6, R6)
    R6[N_DP - 1] = S6[...]
    recv(None, *[
        (f"sc{dm}{ds}", SCB.at[((m + 4 - dm) % 4) * 2 + (s + ds) % 2])
        for dm in range(4) for ds in range(2) if dm or ds
    ])
    chosen = (SCB[0] + SCB[2] + SCB[4] + SCB[6]) / 4
    rejected = (SCB[1] + SCB[3] + SCB[5] + SCB[7]) / 4
    spread = jax.nn.sigmoid(rejected - chosen)
    direction = jnp.where(is0, -spread, spread)
    landed("e6", R6)
    for j in range(N_DP):
        X6[j : j + 1, :] = R6[j]
    back = jnp.zeros((N_DP, HS), F32)
    for t in range(4):
        span = slice(t * 1024, (t + 1) * 1024)
        back = back + nt(X6[:, span].astype(BF16), WO1[:, span])
    for j in range(N_DP):
        T7[j] = back[j : j + 1, :]
    exchange("e7", lambda peer, slot: T7.at[slot], R7)
    R7[N_DP - 1] = T7[N_DP - 1]
    landed("e7", R7)
    for h in range(HEADS):
        DC[h : h + 1, :] = R7[slot_of(h)]
    d_ctx = (DC[...] * direction).astype(BF16)
    d_probs = nt(d_ctx, VC[...])
    leaned = weights1 * d_probs
    d_logits = (leaned - weights1 * jnp.sum(leaned, -1, keepdims=True)) * SCALE
    d_logits = d_logits.astype(BF16)
    d_query = mm(d_logits, KC[...]).astype(BF16).astype(F32)
    for h in range(HEADS):
        S8[:, h * HS : (h + 1) * HS] = d_query[h : h + 1, :]
    lane = lax.broadcasted_iota(jnp.int32, (1, HS), 1)
    meta = jnp.where(lane == 0, direction, jnp.where(lane == 1, chosen, rejected))
    S8[:, HEADS * HS :] = jnp.where(lane == 3, route[0].astype(F32), meta)
    exchange("e8", lambda peer, slot: S8, R8)
    R8[N_DP - 1] = S8[...]
    d_key = tn(d_logits, q_last)
    d_value = tn(probs1, d_ctx)
    for g in range(RING):
        DKV[:, g * HS : (g + 1) * HS] = d_key[g * SEQ : (g + 1) * SEQ, :].astype(BF16)
        DKV[:, (RING + g) * HS : (RING + g + 1) * HS] = d_value[g * SEQ : (g + 1) * SEQ, :].astype(BF16)

    @pl.loop(0, N_DP)
    def _(j):
        span = pl.ds(pl.multiple_of(j * BLK, BLK), BLK)
        GN[:, span] = nt(DKV[...], WKV1[j % RING, j // RING])

    landed("e8", R8)
    for j in range(N_DP):
        X8[j : j + 1, :] = R8[j, :, : HEADS * HS]
    back = nt(X8[...].astype(BF16), WQ1[...])
    for j in range(N_DP):
        T9[j] = back[j : j + 1, :]
    exchange("e9", lambda peer, slot: T9.at[slot], R9)
    R9[N_DP - 1] = T9[N_DP - 1]
    answer = jnp.zeros((1, HS), F32)
    for j in range(N_DP):
        extra = R8[j, :, HEADS * HS :]
        answer = answer + jnp.where(extra[:, 3:4] == dp.astype(F32), extra, 0.0)
        GC[s, j : j + 1, :] = R6[j] * extra[:, 0:1]
    scores_out[...] = answer[:, 1:3]
    XC[s] = X3[...]
    send(is0, ("xc", XC.at[0], XC.at[0], {"section": 1}), ("gc", GC.at[0], GC.at[0], {"section": 1}))
    landed("e9", R9)
    for h in range(N_DP):
        GNL[:, h * BLK : (h + 1) * BLK] = R9[slot_of(h)]

    HL[...] = (toward * direction[:, 0:1]).astype(BF16).astype(F32)
    NL[...] = jnp.zeros_like(NL)

    @pl.loop(0, 4)
    def _(g):
        part = pl.ds(pl.multiple_of(g * 16, 16), 16)
        rows = H1[part, :].astype(F32)
        scale = lax.rsqrt(jnp.mean(rows * rows, -1, keepdims=True) + EPS)
        unit = rows * scale
        last = last_rows(g)
        d_normed = GN[part, :] + jnp.where(last, GNL[...], 0.0)
        NL[...] += jnp.sum(d_normed * unit, 0, keepdims=True)
        pulled = d_normed * GA[1]
        d_rows = scale * (pulled - unit * jnp.mean(pulled * unit, -1, keepdims=True))
        G[pl.ds(pl.multiple_of(z * SEQ + g * 16, 16), 16), :] = (
            d_rows + jnp.where(last, HL[...], 0.0)
        ).astype(BF16)

    ring_z1("g", G)
    across = pl.ds(pl.multiple_of(other * HALF, HALF), HALF)

    def to_core(tag, zz):
        send(None, (tag, G.at[my_rows(zz), across], GP.at[my_rows(zz)], {"section": other}))

    to_core("gp0", z)

    recv(is1, ("xc", XC.at[0]), ("gc", GC.at[0]))

    @pl.when(is1)
    def _():
        rows_a, rows_b = XC[0].astype(BF16), XC[1].astype(BF16)

        @pl.loop(0, 8)
        def _(t):
            span = pl.ds(pl.multiple_of(t * 512, 512), 512)
            grad_out[0, 0, :, span] = tn(rows_a, GC[0, :, span].astype(BF16)) + tn(
                rows_b, GC[1, :, span].astype(BF16)
            )

    for h in range(N_DP):
        SG[h, :, BLK:] = NL[:, h * BLK : (h + 1) * BLK]

    ring_z2("g", G)
    to_core("gp1", zl)
    to_core("gp2", zr)
    ring_z3("g", G)
    to_core("gp3", zo)

    recv(None, ("ctt", CTP), ("gp0", GP.at[my_rows(z)]), ("gp1", GP.at[my_rows(zl)]),
         ("gp2", GP.at[my_rows(zr)]), ("gp3", GP.at[my_rows(zo)]))

    @pl.loop(0, 4)
    def _(t):
        span = pl.ds(pl.multiple_of(t * 512, 512), 512)
        here = pl.ds(pl.multiple_of(s * HALF + t * 512, 512), 512)
        GOP[:, span] = (mm(CTT[...], G[:, here]) + mm(CTP[...], GP[:, span])).astype(BF16)

    def head_rows(yy):
        return GOP.at[pl.ds(pl.multiple_of(yy * HS, HS), HS)]

    def head_half(yy, half):
        return GOP.at[pl.ds(pl.multiple_of(yy * HS + half * 64, 64), 64)]

    send(None, ("r1r", head_half(yo, 0), FWD2.at[0], {"dp": at_yr}),
         ("r1l", head_half(yo, 1), FWD2.at[1], {"dp": at_yl}))
    send(is1, ("rc", head_rows(y), LAND2.at[4], {"section": 0}))

    DCT[...] = jnp.zeros_like(DCT)

    @pl.loop(0, 8)
    def _(t):
        span = pl.ds(pl.multiple_of(t * 512, 512), 512)
        DCT[...] += nt(G[:, span], WO[:, span])

    for side, tag, dest, at in ((0, "r1r", yr, at_yr), (1, "r1l", yl, at_yl)):
        recv(None, (tag, FWD2.at[side]))
        rows = pl.ds(pl.multiple_of(dest * HS + side * 64, 64), 64)
        GOP[rows, :] = (GOP[rows, :].astype(F32) + FWD2[side].astype(F32)).astype(BF16)
        send(is0, (f"ra{side}", head_rows(dest), LAND2.at[side], {"dp": at, "section": 0}))
        send(is1, (f"rb{side}", head_rows(dest), LAND2.at[2 + side], {"dp": at, "section": 0}))

    d_key = jnp.zeros((ROWS, HS), F32)
    d_value = jnp.zeros((ROWS, HS), F32)
    for h in range(GROUP):
        span = slice(h * HS, (h + 1) * HS)
        d_ctx = DCT[:, span].astype(BF16)
        weights = WA[h]
        leaned = weights * nt(d_ctx, KVB[:, HS:])
        d_logits = (leaned - weights * jnp.sum(leaned, -1, keepdims=True)) * SCALE
        d_logits = d_logits.astype(BF16)
        DQB[:, span] = mm(d_logits, KVB[:, :HS]).astype(BF16)
        d_key = d_key + tn(d_logits, QB[:, span])
        d_value = d_value + tn(weights.astype(BF16), d_ctx)
    DKVB[:, :HS] = d_key.astype(BF16)
    DKVB[:, HS:] = d_value.astype(BF16)

    @pl.loop(0, N_DP)
    def _(j):
        span = pl.ds(pl.multiple_of(j * BLK, BLK), BLK)
        yy, zz = j % RING, j // RING
        d_normed = nt(DQB[...], WQ[yy, zz]) + nt(DKVB[...], WKV[yy, zz])
        sums = jnp.sum(d_normed * N[:, span].astype(F32), 0, keepdims=True)
        SG[j, :, :BLK] = sums / GA[0, :, span]

    exchange("e10", lambda peer, slot: SG.at[peer], RG)
    RG[N_DP - 1] = SG[dp]
    landed("e10", RG)
    total = RG[0]
    for j in range(1, N_DP):
        total = total + RG[j]
    SP[...] = total
    send(None, ("sp", SP, PG, {"section": other}))

    recv(is0, ("rc", LAND2.at[4]), ("ra0", LAND2.at[0]), ("ra1", LAND2.at[1]),
         ("rb0", LAND2.at[2]), ("rb1", LAND2.at[3]))
    recv(None, ("sp", PG))
    both = total + PG[...]
    gain_out[0] = jnp.where(is0, both[:, :BLK], both[:, BLK:])

    @pl.when(is0)
    def _():
        @pl.loop(0, 8)
        def _(g):
            part = pl.ds(pl.multiple_of(g * 16, 16), 16)
            own = pl.ds(pl.multiple_of(y * HS + g * 16, 16), 16)
            grad_out[0, 0, part, pl.ds(0, HALF)] = GOP[own, :].astype(F32) + (
                LAND2[0, part, :].astype(F32) + LAND2[1, part, :].astype(F32)
            )
            grad_out[0, 0, part, pl.ds(HALF, HALF)] = LAND2[4, part, :].astype(F32) + (
                LAND2[2, part, :].astype(F32) + LAND2[3, part, :].astype(F32)
            )

    for cond, fin in pending:
        guarded(cond, fin)
    assert len(ids) <= N_SEMS, len(ids)


def body(embeds, lengths, route, w_query, w_keyval, w_out, norm_gain, head):
    hbm = pl.BlockSpec(memory_space=pl.ANY)
    vmem = pl.BlockSpec(memory_space=pltpu.VMEM)
    smem = pl.BlockSpec(memory_space=pltpu.SMEM)
    V = pltpu.VMEM
    row = lambda n: V((1, n), F32)
    slots = lambda n: V((N_DP, 1, n), F32)
    scratch = [
        V((SEQ, D), BF16), V((2, 1, D), F32), row(D), V((ROWS, D), BF16),
        V((RING, RING, BLK, QW), BF16), V((RING, RING, BLK, 2 * HS), BF16), V((QW, D), BF16),
        V((BLK, HEADS * HS), BF16), V((HS, D), BF16), V((RING, RING, BLK, 2 * RING * HS), BF16),
        V((ROWS, QW), F32), V((ROWS, 2 * HS), F32), V((ROWS, QW), BF16), V((ROWS, 2 * HS), BF16),
        V((GROUP, ROWS, ROWS), F32), V((ROWS, QW), BF16), V((QW, ROWS), BF16), V((QW, ROWS), BF16),
        V((ROWS, D), BF16), V((2, 32, D), BF16), V((2, SEQ, D), BF16),
        V((SEQ, D), BF16), V((SEQ, D), BF16), V((SEQ, 2 * RING * HS), F32),
        V((RING * SEQ, HS), BF16), V((RING * SEQ, HS), BF16), V((HEADS, HS), F32),
        row(D), row(D), slots(BLK), slots(BLK), V((N_DP, BLK), F32), slots(HEADS * HS), slots(HEADS * HS),
        slots(HS), slots(HS), V((N_DP, HS), F32), slots(D), slots(D), V((8, 1, HS), F32),
        row(D), slots(D), V((N_DP, D), F32), slots(HS), slots(HS), V((HEADS, HS), F32),
        row(HEADS * HS + HS), slots(HEADS * HS + HS), V((N_DP, HEADS * HS), F32), slots(BLK), slots(BLK),
        row(D), V((2, N_DP, HS), F32), V((2, N_DP, D), F32), V((SEQ, D), F32), V((SEQ, 2 * RING * HS), BF16),
        V((ROWS, D), BF16), V((ROWS, HALF), BF16), V((ROWS, QW), F32), V((ROWS, QW), BF16),
        V((ROWS, 2 * HS), BF16), V((QW, HALF), BF16), V((2, 64, HALF), BF16), V((5, HS, HALF), BF16),
        slots(2 * BLK), slots(2 * BLK), row(2 * BLK), row(2 * BLK),
        pltpu.SemaphoreType.DMA((N_SEMS,)), pltpu.SemaphoreType.DMA((N_SEMS,)), pltpu.SemaphoreType.DMA((8,)),
    ]
    return pl.pallas_call(
        kernel,
        out_shape=(
            jax.ShapeDtypeStruct((1, 2), F32),
            jax.ShapeDtypeStruct((1, 1, HS, D), F32),
            jax.ShapeDtypeStruct((1, 1, BLK), F32),
        ),
        in_specs=[hbm, smem, smem, hbm, hbm, hbm, hbm, hbm],
        out_specs=(vmem, vmem, vmem),
        scratch_shapes=scratch,
        compiler_params=pltpu.CompilerParams(
            collective_id=0, has_side_effects=True, vmem_limit_bytes=60 * 1024 * 1024
        ),
    )(embeds, lengths, route, w_query, w_keyval, w_out, norm_gain, head)


def solution(mesh):
    placed = (
        P("member", "dp", None, None, None),
        P("dp", None),
        P("dp"),
        P("member", "section", "dp", None),
        P("member", "section", "dp", None),
        P("member", "section", "dp", None),
        P("member", "section", None),
        P("member", None),
    )
    return jax.shard_map(
        body,
        mesh=mesh,
        in_specs=placed,
        out_specs=(P("dp", None), P("member", "section", "dp", None), P("member", "section", "dp")),
        check_vma=False,
    )
```

```python
import jax
import jax.numpy as jnp
from jax import lax
from jax.experimental import pallas as pl
from jax.experimental.pallas import tpu as pltpu
from jax.sharding import PartitionSpec as P

MESH = pl.DeviceIdType.MESH
F32 = jnp.float32
BF16 = jnp.bfloat16
EPS = 1e-05
HS = 128
SEQ = 64
D = 4096
RING = 4
N_DP = RING * RING
HEADS = 16
GROUP = HEADS // RING
QW = GROUP * HS
ROWS = RING * SEQ
BLK = D // N_DP
HALF = D // 2
SCALE = HS ** (-0.5)
N_SEMS = 160


def mm(a, b):
    return jnp.dot(a, b, preferred_element_type=F32)


def nt(a, b):
    return lax.dot_general(a, b, (((1,), (1,)), ((), ())), preferred_element_type=F32)


def tn(a, b):
    return lax.dot_general(a, b, (((0,), (0,)), ((), ())), preferred_element_type=F32)


def kernel(
    emb, lens, route, wq, wkv, wo, gain, head,
    scores_out, grad_out, gain_out,
    X, GA, HD, N, W, WO, WQ1, WO1, WKV1,
    QA, QB, WA, CTX, CTT, CTP, OP, FWD, LAND,
    H1, N1, KVA1, KC, VC, Q16,
    NL, HL, S1, R1, X1, T2, R2, S3, R3, X3, T4, R4, SCB, S6, R6, X6, T7, R7, DC,
    S8, R8, X8, T9, R9, GNL, XC, GC, GN, DKV,
    G, GP, DCT, DQB, GOP, FWD2, LAND2, SG, RG, SP, PG,
    ssem, rsem, lsem,
):
    s = lax.axis_index("section")
    m = lax.axis_index("member")
    dp = lax.axis_index("dp")
    z = dp // RING
    y = dp % RING
    other = 1 - s
    zr, zl, zo = (z + 1) % RING, (z + 3) % RING, (z + 2) % RING
    yr, yl, yo = (y + 1) % RING, (y + 3) % RING, (y + 2) % RING
    at_zr, at_zl, at_zo = zr * RING + y, zl * RING + y, zo * RING + y
    at_yr, at_yl = z * RING + yr, z * RING + yl
    is0 = s == 0
    is1 = s == 1
    ids = {}
    pending = []

    def desc(name, src, dst, **dev):
        i = ids.setdefault(name, len(ids))
        return pltpu.make_async_remote_copy(
            src_ref=src, dst_ref=dst, send_sem=ssem.at[i], recv_sem=rsem.at[i],
            device_id=dev, device_id_type=MESH,
        )

    def guarded(cond, act):
        if cond is None:
            act()
        else:
            pl.when(cond)(act)

    def send(cond, *items):
        copies = [desc(name, src, dst, **dev) for name, src, dst, dev in items]

        def act():
            for c in copies:
                c.start()

        guarded(cond, act)

        def fin():
            for c in copies:
                c.wait_send()

        pending.append((cond, fin))

    def recv(cond, *items):
        copies = [desc(name, dst, dst, section=other) for name, dst in items]

        def act():
            for c in copies:
                c.wait_recv()

        guarded(cond, act)

    def exchange(name, src_of, land):
        i = ids.setdefault(name, len(ids))

        @pl.loop(1, N_DP)
        def _(k):
            peer = (dp + k) % N_DP
            pltpu.make_async_remote_copy(
                src_ref=src_of(peer, N_DP - 1 - k), dst_ref=land.at[k - 1],
                send_sem=ssem.at[i], recv_sem=rsem.at[i],
                device_id={"dp": peer}, device_id_type=MESH,
            ).start()

        whole = desc(name, land.at[pl.ds(0, N_DP - 1)], land.at[pl.ds(0, N_DP - 1)], section=other)
        pending.append((None, whole.wait_send))

    def landed(name, land):
        desc(name, land.at[pl.ds(0, N_DP - 1)], land.at[pl.ds(0, N_DP - 1)], section=other).wait_recv()

    def slot_of(h):
        return (dp + N_DP - 1 - h) % N_DP

    lx = pltpu.make_async_copy(emb.at[0, 0, s], X, lsem.at[0])
    lg = pltpu.make_async_copy(gain.at[0], GA.at[s], lsem.at[1])
    lh = pltpu.make_async_copy(head, HD, lsem.at[2])
    lx.start()
    lg.start()
    lh.start()
    wq_mine, wkv_mine, wo_mine = wq.at[0, 0], wkv.at[0, 0], wo.at[0, 0]

    def cols(ref, first, size):
        return ref.at[:, pl.ds(pl.multiple_of(first, HS), size)]

    def slices(dest_z):
        return (
            (cols(wq_mine, dest_z * QW, QW), W.at[y, z, :, pl.ds(0, QW)]),
            (cols(wkv_mine, dest_z * HS, HS), W.at[y, z, :, pl.ds(QW, HS)]),
            (cols(wkv_mine, RING * HS + dest_z * HS, HS), W.at[y, z, :, pl.ds(QW + HS, HS)]),
        )

    wo_rows = lambda yy: WO.at[pl.ds(pl.multiple_of(yy * HS, HS), HS)]
    local0 = [pltpu.make_async_copy(a, b, lsem.at[3 + n]) for n, (a, b) in enumerate(slices(z))]
    local0.append(pltpu.make_async_copy(wo_mine, wo_rows(y), lsem.at[6]))
    local1 = [
        pltpu.make_async_copy(wq_mine, WQ1, lsem.at[3]),
        pltpu.make_async_copy(wkv_mine, WKV1.at[y, z], lsem.at[4]),
        pltpu.make_async_copy(wo_mine, WO1, lsem.at[5]),
    ]

    @pl.when(is0)
    def _():
        for c in local0:
            c.start()

    @pl.when(is1)
    def _():
        for c in local1:
            c.start()

    barrier = pltpu.get_barrier_semaphore()

    @pl.loop(1, N_DP)
    def _(k):
        pl.semaphore_signal(barrier, inc=1, device_id={"dp": (dp + k) % N_DP}, device_id_type=MESH)

    for dm in range(4):
        for ds in range(2):
            if dm or ds:
                pl.semaphore_signal(
                    barrier, inc=1, device_id={"member": (m + dm) % 4, "section": (s + ds) % 2},
                    device_id_type=MESH,
                )
    for at in (at_yr, at_yl):
        pl.semaphore_signal(barrier, inc=1, device_id={"section": other, "dp": at}, device_id_type=MESH)
    pl.semaphore_wait(barrier, N_DP - 1 + 7 + 2)

    for far, at in ((1, at_zr), (3, at_zl), (2, at_zo)):
        dest = (z + far) % RING
        send(is0, *[(f"a2a{far}{n}", a, b, {"dp": at}) for n, (a, b) in enumerate(slices(dest))])

    def w_out_step(zz, n):
        chunk = W.at[y, zz]
        send(is0, (f"w{n}r", chunk, chunk, {"dp": at_yr}), (f"w{n}l", chunk, chunk, {"dp": at_yl}),
             (f"w{n}c", chunk, chunk, {"section": 1}))

    @pl.when(is0)
    def _():
        for c in local0:
            c.wait()

    @pl.when(is1)
    def _():
        for c in local1:
            c.wait()

    w_out_step(z, 0)
    LO, HI = pl.ds(0, 128), pl.ds(128, 128)
    b_own = WKV1.at[y, z, HI]
    send(is1, ("byr", b_own, b_own, {"dp": at_yr}), ("byl", b_own, b_own, {"dp": at_yl}))
    send(None, ("gain", gain.at[0], GA.at[s], {"section": other}))

    lx.wait()
    lg.wait()
    lh.wait()
    recv(None, ("gain", GA.at[other]))
    my_rows = lambda zz: pl.ds(pl.multiple_of(zz * SEQ, SEQ), SEQ)

    @pl.loop(0, 4)
    def _(g):
        part = pl.ds(pl.multiple_of(g * 16, 16), 16)
        rows = X[part, :].astype(F32)
        unit = rows * lax.rsqrt(jnp.mean(rows * rows, -1, keepdims=True) + EPS)
        N[pl.ds(pl.multiple_of(z * SEQ + g * 16, 16), 16), :] = (unit * GA[0]).astype(BF16)

    def half_rows(ref, zz, half):
        return ref.at[pl.ds(pl.multiple_of(zz * SEQ + half * 32, 32), 32)]

    def ring_z1(name, ref):
        block = ref.at[my_rows(z)]
        send(None, (name + "r", block, block, {"dp": at_zr}), (name + "l", block, block, {"dp": at_zl}))

    def ring_z2(name, ref):
        recv(None, (name + "r", ref.at[my_rows(zl)]))
        a = half_rows(ref, zl, 0)
        send(None, (name + "R", a, a, {"dp": at_zr}))
        recv(None, (name + "l", ref.at[my_rows(zr)]))
        b = half_rows(ref, zr, 1)
        send(None, (name + "L", b, b, {"dp": at_zl}))

    def ring_z3(name, ref):
        recv(None, (name + "R", half_rows(ref, zo, 0)), (name + "L", half_rows(ref, zo, 1)))

    ring_z1("n", N)

    order = (z, zl, zr, zo)
    for n, far in ((1, 1), (2, 3), (3, 2)):
        zz = order[n]
        recv(is0, (f"a2a{far}0", W.at[y, zz, :, pl.ds(0, QW)]),
             (f"a2a{far}1", W.at[y, zz, :, pl.ds(QW, HS)]),
             (f"a2a{far}2", W.at[y, zz, :, pl.ds(QW + HS, HS)]))
        w_out_step(zz, n)
    b_half = lambda yy, half: WKV1.at[yy, z, pl.ds(128 + 64 * half, 64)]
    recv(is1, ("byr", WKV1.at[yl, z, HI]))
    send(is1, ("byR", b_half(yl, 0), b_half(yl, 0), {"dp": at_yr}))
    recv(is1, ("byl", WKV1.at[yr, z, HI]))
    send(is1, ("byL", b_half(yr, 1), b_half(yr, 1), {"dp": at_yl}))
    ring_z2("n", N)
    a_own = WKV1.at[y, z, LO]
    send(is1, ("azr", a_own, a_own, {"dp": at_zr}), ("azl", a_own, a_own, {"dp": at_zl}))
    recv(is1, ("byR", b_half(yo, 0)), ("byL", b_half(yo, 1)))
    b_item = lambda zz: WKV1.at[:, zz, HI]
    send(is1, ("bzr", b_item(z), b_item(z), {"dp": at_zr}), ("bzl", b_item(z), b_item(z), {"dp": at_zl}),
         ("bc", b_item(z), b_item(z), {"section": 0}))

    for side, yy, fwd, at, kept in (("r", yl, "R", at_yr, (0, 2)), ("l", yr, "L", at_yl, (1, 3))):
        for n in range(RING):
            chunk = W.at[yy, order[n]]
            recv(is0, (f"w{n}{side}", chunk))
            if n in kept:
                send(is0, (f"w{n}{fwd}", chunk, chunk, {"dp": at}))
            send(is0, (f"w{n}c{side}", chunk, chunk, {"section": 1}))
    mine = wo_rows(y)
    send(is0,
         ("wo_r", mine, mine, {"dp": at_yr}),
         ("wo_l", mine, mine, {"dp": at_yl}),
         ("wo_c", mine, mine, {"section": 1}))

    a_half = lambda zz, half: WKV1.at[y, zz, pl.ds(64 * half, 64)]
    recv(is1, ("azr", WKV1.at[y, zl, LO]))
    send(is1, ("azR", a_half(zl, 0), a_half(zl, 0), {"dp": at_zr}))
    recv(is1, ("azl", WKV1.at[y, zr, LO]))
    send(is1, ("azL", a_half(zr, 1), a_half(zr, 1), {"dp": at_zl}))

    QA[...] = jnp.zeros_like(QA)

    def project(yy):
        @pl.loop(0, RING)
        def _(zz):
            block = N[:, pl.ds(pl.multiple_of((zz * RING + yy) * BLK, BLK), BLK)]
            QA[...] += mm(block, W[yy, zz])

    def w_core(tag, yy):
        recv(is1, *[(f"w{n}c{tag}", W.at[yy, order[n]]) for n in range(RING)])

    ring_z3("n", N)
    w_core("", y)
    project(y)
    w_core("r", yl)
    project(yl)
    w_core("l", yr)
    project(yr)
    b_two = lambda zz, half: WKV1.at[pl.ds(2 * half, 2), zz, HI]
    recv(is1, ("bzr", b_item(zl)))
    send(is1, ("bzR", b_two(zl, 0), b_two(zl, 0), {"dp": at_zr}),
         ("bcr", b_item(zl), b_item(zl), {"section": 0}))
    recv(is1, ("bzl", b_item(zr)))
    send(is1, ("bzL", b_two(zr, 1), b_two(zr, 1), {"dp": at_zl}),
         ("bcl", b_item(zr), b_item(zr), {"section": 0}))
    for n, fwd in ((0, "R"), (1, "L"), (2, "R"), (3, "L")):
        chunk = W.at[yo, order[n]]
        recv(is0, (f"w{n}{fwd}", chunk))
        send(is0, (f"w{n}co", chunk, chunk, {"section": 1}))

    def wo_half(yy, half):
        return WO.at[pl.ds(pl.multiple_of(yy * HS + half * 64, 64), 64)]

    w_core("o", yo)
    project(yo)
    QB[...] = QA[...].astype(BF16)
    recv(is0, ("wo_r", wo_rows(yl)))
    send(is0, ("wo_R", wo_half(yl, 0), wo_half(yl, 0), {"dp": at_yr}),
         ("wo_cl", wo_rows(yl), wo_rows(yl), {"section": 1}))
    recv(is0, ("wo_l", wo_rows(yr)))
    send(is0, ("wo_L", wo_half(yr, 1), wo_half(yr, 1), {"dp": at_yl}),
         ("wo_cr", wo_rows(yr), wo_rows(yr), {"section": 1}))
    recv(is1, ("azR", a_half(zo, 0)), ("azL", a_half(zo, 1)))
    a_item = lambda yy: WKV1.at[yy, :, LO]
    send(is1, ("ayr", a_item(y), a_item(y), {"dp": at_yr}), ("ayl", a_item(y), a_item(y), {"dp": at_yl}),
         ("ac", a_item(y), a_item(y), {"section": 0}))

    r_i = lax.broadcasted_iota(jnp.int32, (ROWS, ROWS), 0)
    c_i = lax.broadcasted_iota(jnp.int32, (ROWS, ROWS), 1)
    seen = jnp.logical_and(r_i // SEQ == c_i // SEQ, c_i <= r_i)
    for h in range(GROUP):
        span = slice(h * HS, (h + 1) * HS)
        logits = nt(QB[:, span], QB[:, QW : QW + HS]) * SCALE
        grown = jnp.where(seen, jnp.exp(jnp.where(seen, logits, 0.0)), 0.0)
        weights = grown / jnp.sum(grown, -1, keepdims=True)
        WA[h] = weights
        context = mm(weights.astype(BF16), QB[:, QW + HS :])
        CTX[:, span] = context.astype(BF16)
        CTT[span, :] = context.T.astype(BF16)
    send(None, ("ctt", CTT, CTP, {"section": other}))
    send(is1, ("q1", WQ1, WQ1, {"section": 0}), ("o1", WO1, WO1, {"section": 0}))

    recv(is0, ("wo_R", wo_half(yo, 0)), ("wo_L", wo_half(yo, 1)))
    send(is0, ("wo_co", wo_rows(yo), wo_rows(yo), {"section": 1}))
    recv(is1, ("wo_c", wo_rows(y)), ("wo_cl", wo_rows(yl)), ("wo_cr", wo_rows(yr)), ("wo_co", wo_rows(yo)))

    @pl.loop(0, 8)
    def _(t):
        span = pl.ds(pl.multiple_of(t * 512, 512), 512)
        OP[:, span] = mm(CTX[...], WO[:, span]).astype(BF16)

    send(None, ("o1r", half_rows(OP, zo, 0), FWD.at[0], {"dp": at_zr}),
         ("o1l", half_rows(OP, zo, 1), FWD.at[1], {"dp": at_zl}))
    for side, tag, dest, at in ((0, "o1r", zr, at_zr), (1, "o1l", zl, at_zl)):
        recv(None, (tag, FWD.at[side]))

        @pl.loop(0, 2)
        def _(g):
            rows = pl.ds(pl.multiple_of(dest * SEQ + side * 32 + g * 16, 16), 16)
            part = pl.ds(pl.multiple_of(g * 16, 16), 16)
            OP[rows, :] = (OP[rows, :].astype(F32) + FWD[side, part, :].astype(F32)).astype(BF16)

        send(None, (f"o2{side}", OP.at[my_rows(dest)], LAND.at[side], {"dp": at}))

    a_two = lambda yy, half: WKV1.at[yy, pl.ds(2 * half, 2), LO]
    recv(is1, ("bzR", b_two(zo, 0)), ("bzL", b_two(zo, 1)))
    send(is1, ("bco", b_item(zo), b_item(zo), {"section": 0}))
    for tag, yy, fwd, half, at in (("r", yl, "R", 0, at_yr), ("l", yr, "L", 1, at_yl)):
        recv(is1, ("ay" + tag, a_item(yy)))
        send(is1, ("ay" + fwd, a_two(yy, half), a_two(yy, half), {"dp": at}),
             ("ac" + tag, a_item(yy), a_item(yy), {"section": 0}))

    recv(None, ("o20", LAND.at[0]), ("o21", LAND.at[1]))

    length = jnp.where(is0, lens[0, 0], lens[0, 1])
    NL[...] = jnp.zeros_like(NL)
    HL[...] = jnp.zeros_like(HL)

    def last_rows(g):
        return lax.broadcasted_iota(jnp.int32, (16, D), 0) + g * 16 == length - 1

    @pl.loop(0, 4)
    def _(g):
        part = pl.ds(pl.multiple_of(g * 16, 16), 16)
        own = pl.ds(pl.multiple_of(z * SEQ + g * 16, 16), 16)
        total = X[part, :].astype(F32) + (
            OP[own, :].astype(F32) + LAND[0, part, :].astype(F32) + LAND[1, part, :].astype(F32)
        )
        hidden = total.astype(BF16)
        H1[part, :] = hidden
        rows = hidden.astype(F32)
        unit = rows * lax.rsqrt(jnp.mean(rows * rows, -1, keepdims=True) + EPS)
        normed = (unit * GA[1]).astype(BF16)
        N1[part, :] = normed
        last = last_rows(g)
        NL[...] += jnp.sum(jnp.where(last, normed.astype(F32), 0.0), 0, keepdims=True)
        HL[...] += jnp.sum(jnp.where(last, rows, 0.0), 0, keepdims=True)

    for j in range(N_DP):
        S1[j] = NL[:, j * BLK : (j + 1) * BLK]
    exchange("e1", lambda peer, slot: S1.at[peer], R1)
    R1[N_DP - 1] = S1[dp]
    KVA1[...] = jnp.zeros_like(KVA1)

    def project1(yy):
        @pl.loop(0, RING)
        def _(zz):
            block = N1[:, pl.ds(pl.multiple_of((zz * RING + yy) * BLK, BLK), BLK)]
            KVA1[...] += mm(block, WKV1[yy, zz])

    recv(is0, ("q1", WQ1), ("o1", WO1), ("ac", a_item(y)),
         ("bc", b_item(z)), ("bcr", b_item(zl)), ("bcl", b_item(zr)), ("bco", b_item(zo)))
    project1(y)
    landed("e1", R1)
    for j in range(N_DP):
        X1[j : j + 1, :] = R1[j]
    back = mm(X1[...].astype(BF16), WQ1[...])
    for j in range(N_DP):
        T2[j] = back[j : j + 1, :]
    exchange("e2", lambda peer, slot: T2.at[slot], R2)
    R2[N_DP - 1] = T2[N_DP - 1]
    for tag, yy in (("r", yl), ("l", yr)):
        recv(is0, ("ac" + tag, a_item(yy)))
        project1(yy)
    recv(is1, ("ayR", a_two(yo, 0)), ("ayL", a_two(yo, 1)))
    send(is1, ("aco", a_item(yo), a_item(yo), {"section": 0}))
    recv(is0, ("aco", a_item(yo)))
    project1(yo)
    for g in range(RING):
        KC[g * SEQ : (g + 1) * SEQ, :] = KVA1[:, g * HS : (g + 1) * HS].astype(BF16)
        VC[g * SEQ : (g + 1) * SEQ, :] = KVA1[:, (RING + g) * HS : (RING + g + 1) * HS].astype(BF16)
    landed("e2", R2)
    q_row = R2[0]
    for j in range(1, N_DP):
        q_row = q_row + R2[j]
    for h in range(HEADS):
        Q16[h : h + 1, :] = q_row[:, h * HS : (h + 1) * HS]
    q_last = Q16[...].astype(BF16)

    h_i = lax.broadcasted_iota(jnp.int32, (HEADS, RING * SEQ), 0)
    k_i = lax.broadcasted_iota(jnp.int32, (HEADS, RING * SEQ), 1)
    seen1 = jnp.logical_and(h_i // GROUP == k_i // SEQ, k_i % SEQ < length)
    logits = nt(q_last, KC[...]) * SCALE
    grown = jnp.where(seen1, jnp.exp(jnp.where(seen1, logits, 0.0)), 0.0)
    weights1 = grown / jnp.sum(grown, -1, keepdims=True)
    probs1 = weights1.astype(BF16)
    context1 = mm(probs1, VC[...]).astype(BF16).astype(F32)
    for h in range(HEADS):
        S3[h] = context1[h : h + 1, :]
    exchange("e3", lambda peer, slot: S3.at[peer], R3)
    R3[N_DP - 1] = S3[dp]
    landed("e3", R3)
    for j in range(N_DP):
        X3[j : j + 1, :] = R3[j]
    x3 = X3[...].astype(BF16)
    for t in range(4):
        back = mm(x3, WO1[:, t * 1024 : (t + 1) * 1024])
        for j in range(N_DP):
            T4[j, :, t * 1024 : (t + 1) * 1024] = back[j : j + 1, :]
    exchange("e4", lambda peer, slot: T4.at[slot], R4)
    R4[N_DP - 1] = T4[N_DP - 1]
    landed("e4", R4)
    update = R4[0]
    for j in range(1, N_DP):
        update = update + R4[j]
    final = (HL[...] + update).astype(BF16).astype(F32)

    scale1 = lax.rsqrt(jnp.mean(final * final, -1, keepdims=True) + EPS)
    unit1 = final * scale1
    weighed = unit1 * HD[...]
    score = jnp.sum(weighed, -1, keepdims=True)
    mine_sc = m * 2 + s
    SCB[mine_sc] = jnp.broadcast_to(score, (1, HS))
    send(None, *[
        (f"sc{dm}{ds}", SCB.at[mine_sc], SCB.at[mine_sc], {"member": (m + dm) % 4, "section": (s + ds) % 2})
        for dm in range(4) for ds in range(2) if dm or ds
    ])
    toward = scale1 * (HD[...] - unit1 * (score / D))
    S6[...] = toward.astype(BF16).astype(F32)
    exchange("e6", lambda peer, slot: S6, R6)
    R6[N_DP - 1] = S6[...]
    recv(None, *[
        (f"sc{dm}{ds}", SCB.at[((m + 4 - dm) % 4) * 2 + (s + ds) % 2])
        for dm in range(4) for ds in range(2) if dm or ds
    ])
    chosen = (SCB[0] + SCB[2] + SCB[4] + SCB[6]) / 4
    rejected = (SCB[1] + SCB[3] + SCB[5] + SCB[7]) / 4
    spread = jax.nn.sigmoid(rejected - chosen)
    direction = jnp.where(is0, -spread, spread)
    landed("e6", R6)
    for j in range(N_DP):
        X6[j : j + 1, :] = R6[j]
    back = jnp.zeros((N_DP, HS), F32)
    for t in range(4):
        span = slice(t * 1024, (t + 1) * 1024)
        back = back + nt(X6[:, span].astype(BF16), WO1[:, span])
    for j in range(N_DP):
        T7[j] = back[j : j + 1, :]
    exchange("e7", lambda peer, slot: T7.at[slot], R7)
    R7[N_DP - 1] = T7[N_DP - 1]
    landed("e7", R7)
    for h in range(HEADS):
        DC[h : h + 1, :] = R7[slot_of(h)]
    d_ctx = (DC[...] * direction).astype(BF16)
    d_probs = nt(d_ctx, VC[...])
    leaned = weights1 * d_probs
    d_logits = (leaned - weights1 * jnp.sum(leaned, -1, keepdims=True)) * SCALE
    d_logits = d_logits.astype(BF16)
    d_query = mm(d_logits, KC[...]).astype(BF16).astype(F32)
    for h in range(HEADS):
        S8[:, h * HS : (h + 1) * HS] = d_query[h : h + 1, :]
    lane = lax.broadcasted_iota(jnp.int32, (1, HS), 1)
    meta = jnp.where(lane == 0, direction, jnp.where(lane == 1, chosen, rejected))
    S8[:, HEADS * HS :] = jnp.where(lane == 3, route[0].astype(F32), meta)
    exchange("e8", lambda peer, slot: S8, R8)
    R8[N_DP - 1] = S8[...]
    d_key = tn(d_logits, q_last)
    d_value = tn(probs1, d_ctx)
    for g in range(RING):
        DKV[:, g * HS : (g + 1) * HS] = d_key[g * SEQ : (g + 1) * SEQ, :].astype(BF16)
        DKV[:, (RING + g) * HS : (RING + g + 1) * HS] = d_value[g * SEQ : (g + 1) * SEQ, :].astype(BF16)

    @pl.loop(0, N_DP)
    def _(j):
        span = pl.ds(pl.multiple_of(j * BLK, BLK), BLK)
        GN[:, span] = nt(DKV[...], WKV1[j % RING, j // RING])

    landed("e8", R8)
    for j in range(N_DP):
        X8[j : j + 1, :] = R8[j, :, : HEADS * HS]
    back = nt(X8[...].astype(BF16), WQ1[...])
    for j in range(N_DP):
        T9[j] = back[j : j + 1, :]
    exchange("e9", lambda peer, slot: T9.at[slot], R9)
    R9[N_DP - 1] = T9[N_DP - 1]
    answer = jnp.zeros((1, HS), F32)
    for j in range(N_DP):
        extra = R8[j, :, HEADS * HS :]
        answer = answer + jnp.where(extra[:, 3:4] == dp.astype(F32), extra, 0.0)
        GC[s, j : j + 1, :] = R6[j] * extra[:, 0:1]
    scores_out[...] = answer[:, 1:3]
    XC[s] = X3[...]
    send(is0, ("xc", XC.at[0], XC.at[0], {"section": 1}), ("gc", GC.at[0], GC.at[0], {"section": 1}))
    landed("e9", R9)
    for h in range(N_DP):
        GNL[:, h * BLK : (h + 1) * BLK] = R9[slot_of(h)]

    HL[...] = (toward * direction[:, 0:1]).astype(BF16).astype(F32)
    NL[...] = jnp.zeros_like(NL)

    @pl.loop(0, 4)
    def _(g):
        part = pl.ds(pl.multiple_of(g * 16, 16), 16)
        rows = H1[part, :].astype(F32)
        scale = lax.rsqrt(jnp.mean(rows * rows, -1, keepdims=True) + EPS)
        unit = rows * scale
        last = last_rows(g)
        d_normed = GN[part, :] + jnp.where(last, GNL[...], 0.0)
        NL[...] += jnp.sum(d_normed * unit, 0, keepdims=True)
        pulled = d_normed * GA[1]
        d_rows = scale * (pulled - unit * jnp.mean(pulled * unit, -1, keepdims=True))
        G[pl.ds(pl.multiple_of(z * SEQ + g * 16, 16), 16), :] = (
            d_rows + jnp.where(last, HL[...], 0.0)
        ).astype(BF16)

    ring_z1("g", G)
    across = pl.ds(pl.multiple_of(other * HALF, HALF), HALF)

    def to_core(tag, zz):
        send(None, (tag, G.at[my_rows(zz), across], GP.at[my_rows(zz)], {"section": other}))

    to_core("gp0", z)

    recv(is1, ("xc", XC.at[0]), ("gc", GC.at[0]))

    @pl.when(is1)
    def _():
        rows_a, rows_b = XC[0].astype(BF16), XC[1].astype(BF16)

        @pl.loop(0, 8)
        def _(t):
            span = pl.ds(pl.multiple_of(t * 512, 512), 512)
            grad_out[0, 0, :, span] = tn(rows_a, GC[0, :, span].astype(BF16)) + tn(
                rows_b, GC[1, :, span].astype(BF16)
            )

    for h in range(N_DP):
        SG[h, :, BLK:] = NL[:, h * BLK : (h + 1) * BLK]

    ring_z2("g", G)
    to_core("gp1", zl)
    to_core("gp2", zr)
    ring_z3("g", G)
    to_core("gp3", zo)

    recv(None, ("ctt", CTP), ("gp0", GP.at[my_rows(z)]), ("gp1", GP.at[my_rows(zl)]),
         ("gp2", GP.at[my_rows(zr)]), ("gp3", GP.at[my_rows(zo)]))

    @pl.loop(0, 4)
    def _(t):
        span = pl.ds(pl.multiple_of(t * 512, 512), 512)
        here = pl.ds(pl.multiple_of(s * HALF + t * 512, 512), 512)
        GOP[:, span] = (mm(CTT[...], G[:, here]) + mm(CTP[...], GP[:, span])).astype(BF16)

    def head_rows(yy):
        return GOP.at[pl.ds(pl.multiple_of(yy * HS, HS), HS)]

    def head_half(yy, half):
        return GOP.at[pl.ds(pl.multiple_of(yy * HS + half * 64, 64), 64)]

    send(None, ("r1r", head_half(yo, 0), FWD2.at[0], {"dp": at_yr}),
         ("r1l", head_half(yo, 1), FWD2.at[1], {"dp": at_yl}))
    send(is1, ("rc", head_rows(y), LAND2.at[4], {"section": 0}))

    DCT[...] = jnp.zeros_like(DCT)

    @pl.loop(0, 8)
    def _(t):
        span = pl.ds(pl.multiple_of(t * 512, 512), 512)
        DCT[...] += nt(G[:, span], WO[:, span])

    for side, tag, dest, at in ((0, "r1r", yr, at_yr), (1, "r1l", yl, at_yl)):
        recv(None, (tag, FWD2.at[side]))
        rows = pl.ds(pl.multiple_of(dest * HS + side * 64, 64), 64)
        GOP[rows, :] = (GOP[rows, :].astype(F32) + FWD2[side].astype(F32)).astype(BF16)
        send(is0, (f"ra{side}", head_rows(dest), LAND2.at[side], {"dp": at, "section": 0}))
        send(is1, (f"rb{side}", head_rows(dest), LAND2.at[2 + side], {"dp": at, "section": 0}))

    d_key = jnp.zeros((ROWS, HS), F32)
    d_value = jnp.zeros((ROWS, HS), F32)
    for h in range(GROUP):
        span = slice(h * HS, (h + 1) * HS)
        d_ctx = DCT[:, span].astype(BF16)
        weights = WA[h]
        leaned = weights * nt(d_ctx, QB[:, QW + HS :])
        d_logits = (leaned - weights * jnp.sum(leaned, -1, keepdims=True)) * SCALE
        d_logits = d_logits.astype(BF16)
        DQB[:, span] = mm(d_logits, QB[:, QW : QW + HS]).astype(BF16)
        d_key = d_key + tn(d_logits, QB[:, span])
        d_value = d_value + tn(weights.astype(BF16), d_ctx)
    DQB[:, QW : QW + HS] = d_key.astype(BF16)
    DQB[:, QW + HS :] = d_value.astype(BF16)

    @pl.loop(0, N_DP)
    def _(j):
        span = pl.ds(pl.multiple_of(j * BLK, BLK), BLK)
        yy, zz = j % RING, j // RING
        d_normed = nt(DQB[...], W[yy, zz])
        sums = jnp.sum(d_normed * N[:, span].astype(F32), 0, keepdims=True)
        SG[j, :, :BLK] = sums / GA[0, :, span]

    exchange("e10", lambda peer, slot: SG.at[peer], RG)
    RG[N_DP - 1] = SG[dp]
    landed("e10", RG)
    total = RG[0]
    for j in range(1, N_DP):
        total = total + RG[j]
    SP[...] = total
    send(None, ("sp", SP, PG, {"section": other}))

    recv(is0, ("rc", LAND2.at[4]), ("ra0", LAND2.at[0]), ("ra1", LAND2.at[1]),
         ("rb0", LAND2.at[2]), ("rb1", LAND2.at[3]))
    recv(None, ("sp", PG))
    both = total + PG[...]
    gain_out[0] = jnp.where(is0, both[:, :BLK], both[:, BLK:])

    @pl.when(is0)
    def _():
        @pl.loop(0, 8)
        def _(g):
            part = pl.ds(pl.multiple_of(g * 16, 16), 16)
            own = pl.ds(pl.multiple_of(y * HS + g * 16, 16), 16)
            grad_out[0, 0, part, pl.ds(0, HALF)] = GOP[own, :].astype(F32) + (
                LAND2[0, part, :].astype(F32) + LAND2[1, part, :].astype(F32)
            )
            grad_out[0, 0, part, pl.ds(HALF, HALF)] = LAND2[4, part, :].astype(F32) + (
                LAND2[2, part, :].astype(F32) + LAND2[3, part, :].astype(F32)
            )

    for cond, fin in pending:
        guarded(cond, fin)
    assert len(ids) <= N_SEMS, len(ids)


def body(embeds, lengths, route, w_query, w_keyval, w_out, norm_gain, head):
    hbm = pl.BlockSpec(memory_space=pl.ANY)
    vmem = pl.BlockSpec(memory_space=pltpu.VMEM)
    smem = pl.BlockSpec(memory_space=pltpu.SMEM)
    V = pltpu.VMEM
    row = lambda n: V((1, n), F32)
    slots = lambda n: V((N_DP, 1, n), F32)
    scratch = [
        V((SEQ, D), BF16), V((2, 1, D), F32), row(D), V((ROWS, D), BF16),
        V((RING, RING, BLK, QW + 2 * HS), BF16), V((QW, D), BF16),
        V((BLK, HEADS * HS), BF16), V((HS, D), BF16), V((RING, RING, BLK, 2 * RING * HS), BF16),
        V((ROWS, QW + 2 * HS), F32), V((ROWS, QW + 2 * HS), BF16),
        V((GROUP, ROWS, ROWS), F32), V((ROWS, QW), BF16), V((QW, ROWS), BF16), V((QW, ROWS), BF16),
        V((ROWS, D), BF16), V((2, 32, D), BF16), V((2, SEQ, D), BF16),
        V((SEQ, D), BF16), V((SEQ, D), BF16), V((SEQ, 2 * RING * HS), F32),
        V((RING * SEQ, HS), BF16), V((RING * SEQ, HS), BF16), V((HEADS, HS), F32),
        row(D), row(D), slots(BLK), slots(BLK), V((N_DP, BLK), F32), slots(HEADS * HS), slots(HEADS * HS),
        slots(HS), slots(HS), V((N_DP, HS), F32), slots(D), slots(D), V((8, 1, HS), F32),
        row(D), slots(D), V((N_DP, D), F32), slots(HS), slots(HS), V((HEADS, HS), F32),
        row(HEADS * HS + HS), slots(HEADS * HS + HS), V((N_DP, HEADS * HS), F32), slots(BLK), slots(BLK),
        row(D), V((2, N_DP, HS), F32), V((2, N_DP, D), F32), V((SEQ, D), F32), V((SEQ, 2 * RING * HS), BF16),
        V((ROWS, D), BF16), V((ROWS, HALF), BF16), V((ROWS, QW), F32), V((ROWS, QW + 2 * HS), BF16),
        V((QW, HALF), BF16), V((2, 64, HALF), BF16), V((5, HS, HALF), BF16),
        slots(2 * BLK), slots(2 * BLK), row(2 * BLK), row(2 * BLK),
        pltpu.SemaphoreType.DMA((N_SEMS,)), pltpu.SemaphoreType.DMA((N_SEMS,)), pltpu.SemaphoreType.DMA((8,)),
    ]
    return pl.pallas_call(
        kernel,
        out_shape=(
            jax.ShapeDtypeStruct((1, 2), F32),
            jax.ShapeDtypeStruct((1, 1, HS, D), F32),
            jax.ShapeDtypeStruct((1, 1, BLK), F32),
        ),
        in_specs=[hbm, smem, smem, hbm, hbm, hbm, hbm, hbm],
        out_specs=(vmem, vmem, vmem),
        scratch_shapes=scratch,
        compiler_params=pltpu.CompilerParams(
            collective_id=0, has_side_effects=True, vmem_limit_bytes=60 * 1024 * 1024
        ),
    )(embeds, lengths, route, w_query, w_keyval, w_out, norm_gain, head)


def solution(mesh):
    placed = (
        P("member", "dp", None, None, None),
        P("dp", None),
        P("dp"),
        P("member", "section", "dp", None),
        P("member", "section", "dp", None),
        P("member", "section", "dp", None),
        P("member", "section", None),
        P("member", None),
    )
    return jax.shard_map(
        body,
        mesh=mesh,
        in_specs=placed,
        out_specs=(P("dp", None), P("member", "section", "dp", None), P("member", "section", "dp")),
        check_vma=False,
    )
```

```python
import jax
import jax.numpy as jnp
from jax import lax
from jax.experimental import pallas as pl
from jax.experimental.pallas import tpu as pltpu
from jax.sharding import PartitionSpec as P

MESH = pl.DeviceIdType.MESH
F32 = jnp.float32
BF16 = jnp.bfloat16
EPS = 1e-05
HS = 128
SEQ = 64
D = 4096
RING = 4
N_DP = RING * RING
HEADS = 16
GROUP = HEADS // RING
QW = GROUP * HS
ROWS = RING * SEQ
BLK = D // N_DP
HALF = D // 2
QUART = D // 4
SCALE = HS ** (-0.5)
N_SEMS = 160


def mm(a, b):
    return jnp.dot(a, b, preferred_element_type=F32)


def nt(a, b):
    return lax.dot_general(a, b, (((1,), (1,)), ((), ())), preferred_element_type=F32)


def tn(a, b):
    return lax.dot_general(a, b, (((0,), (0,)), ((), ())), preferred_element_type=F32)


def kernel(
    emb, lens, route, wq, wkv, wo, gain, head,
    scores_out, grad_out, gain_out,
    X, GA, HD, N, W, WO, WQ1, WO1, WKV1,
    QA, QB, WA, CTX, CTT, CTP, OP, FWD, LAND,
    H1, N1, KVA1, KC, VC, Q16,
    NL, HL, S1, R1, X1, T2, R2, S3, R3, X3, T4, R4, SCB, S6, R6, X6, T7, R7, DC,
    S8, R8, X8, T9, R9, GNL, XC, GC, GN, DKV,
    G, GP, DCT, DQB, GOP, FWD2, LAND2, SG, RG, SP, PG,
    ssem, rsem, lsem,
):
    s = lax.axis_index("section")
    m = lax.axis_index("member")
    dp = lax.axis_index("dp")
    z = dp // RING
    y = dp % RING
    other = 1 - s
    zr, zl, zo = (z + 1) % RING, (z + 3) % RING, (z + 2) % RING
    yr, yl, yo = (y + 1) % RING, (y + 3) % RING, (y + 2) % RING
    at_zr, at_zl, at_zo = zr * RING + y, zl * RING + y, zo * RING + y
    at_yr, at_yl = z * RING + yr, z * RING + yl
    is0 = s == 0
    is1 = s == 1
    ids = {}
    pending = []

    def desc(name, src, dst, **dev):
        i = ids.setdefault(name, len(ids))
        return pltpu.make_async_remote_copy(
            src_ref=src, dst_ref=dst, send_sem=ssem.at[i], recv_sem=rsem.at[i],
            device_id=dev, device_id_type=MESH,
        )

    def guarded(cond, act):
        if cond is None:
            act()
        else:
            pl.when(cond)(act)

    def send(cond, *items):
        copies = [desc(name, src, dst, **dev) for name, src, dst, dev in items]

        def act():
            for c in copies:
                c.start()

        guarded(cond, act)

        def fin():
            for c in copies:
                c.wait_send()

        pending.append((cond, fin))

    def recv(cond, *items):
        copies = [desc(name, dst, dst, section=other) for name, dst in items]

        def act():
            for c in copies:
                c.wait_recv()

        guarded(cond, act)

    def exchange(name, src_of, land):
        i = ids.setdefault(name, len(ids))

        @pl.loop(1, N_DP)
        def _(k):
            peer = (dp + k) % N_DP
            pltpu.make_async_remote_copy(
                src_ref=src_of(peer, N_DP - 1 - k), dst_ref=land.at[k - 1],
                send_sem=ssem.at[i], recv_sem=rsem.at[i],
                device_id={"dp": peer}, device_id_type=MESH,
            ).start()

        whole = desc(name, land.at[pl.ds(0, N_DP - 1)], land.at[pl.ds(0, N_DP - 1)], section=other)
        pending.append((None, whole.wait_send))

    def landed(name, land):
        desc(name, land.at[pl.ds(0, N_DP - 1)], land.at[pl.ds(0, N_DP - 1)], section=other).wait_recv()

    def slot_of(h):
        return (dp + N_DP - 1 - h) % N_DP

    lx = pltpu.make_async_copy(emb.at[0, 0, s], X, lsem.at[0])
    lg = pltpu.make_async_copy(gain.at[0], GA.at[s], lsem.at[1])
    lh = pltpu.make_async_copy(head, HD, lsem.at[2])
    lx.start()
    lg.start()
    lh.start()
    wq_mine, wkv_mine, wo_mine = wq.at[0, 0], wkv.at[0, 0], wo.at[0, 0]

    def cols(ref, first, size):
        return ref.at[:, pl.ds(pl.multiple_of(first, HS), size)]

    def slices(dest_z):
        return (
            (cols(wq_mine, dest_z * QW, QW), W.at[y, z, :, pl.ds(0, QW)]),
            (cols(wkv_mine, dest_z * HS, HS), W.at[y, z, :, pl.ds(QW, HS)]),
            (cols(wkv_mine, RING * HS + dest_z * HS, HS), W.at[y, z, :, pl.ds(QW + HS, HS)]),
        )

    wo_rows = lambda yy: WO.at[pl.ds(pl.multiple_of(yy * HS, HS), HS)]
    local0 = [pltpu.make_async_copy(a, b, lsem.at[3 + n]) for n, (a, b) in enumerate(slices(z))]
    local0.append(pltpu.make_async_copy(wo_mine, wo_rows(y), lsem.at[6]))
    local1 = [
        pltpu.make_async_copy(wq_mine, WQ1, lsem.at[3]),
        pltpu.make_async_copy(wkv_mine, WKV1.at[y, z], lsem.at[4]),
        pltpu.make_async_copy(wo_mine, WO1, lsem.at[5]),
    ]

    @pl.when(is0)
    def _():
        for c in local0:
            c.start()

    @pl.when(is1)
    def _():
        for c in local1:
            c.start()

    barrier = pltpu.get_barrier_semaphore()

    @pl.loop(1, N_DP)
    def _(k):
        pl.semaphore_signal(barrier, inc=1, device_id={"dp": (dp + k) % N_DP}, device_id_type=MESH)

    for dm in range(4):
        for ds in range(2):
            if dm or ds:
                pl.semaphore_signal(
                    barrier, inc=1, device_id={"member": (m + dm) % 4, "section": (s + ds) % 2},
                    device_id_type=MESH,
                )
    for at in (at_yr, at_yl):
        pl.semaphore_signal(barrier, inc=1, device_id={"section": other, "dp": at}, device_id_type=MESH)
    pl.semaphore_wait(barrier, N_DP - 1 + 7 + 2)

    for far, at in ((1, at_zr), (3, at_zl), (2, at_zo)):
        dest = (z + far) % RING
        send(is0, *[(f"a2a{far}{n}", a, b, {"dp": at}) for n, (a, b) in enumerate(slices(dest))])

    def w_out_step(zz, n):
        chunk = W.at[y, zz]
        send(is0, (f"w{n}r", chunk, chunk, {"dp": at_yr}), (f"w{n}l", chunk, chunk, {"dp": at_yl}),
             (f"w{n}c", chunk, chunk, {"section": 1}))

    @pl.when(is0)
    def _():
        for c in local0:
            c.wait()

    @pl.when(is1)
    def _():
        for c in local1:
            c.wait()

    w_out_step(z, 0)
    LO, HI = pl.ds(0, 128), pl.ds(128, 128)
    b_own = WKV1.at[y, z, HI]
    send(is1, ("byr", b_own, b_own, {"dp": at_yr}), ("byl", b_own, b_own, {"dp": at_yl}))
    send(None, ("gain", gain.at[0], GA.at[s], {"section": other}))

    lx.wait()
    lg.wait()
    lh.wait()
    recv(None, ("gain", GA.at[other]))
    my_rows = lambda zz: pl.ds(pl.multiple_of(zz * SEQ, SEQ), SEQ)

    @pl.loop(0, 4)
    def _(g):
        part = pl.ds(pl.multiple_of(g * 16, 16), 16)
        rows = X[part, :].astype(F32)
        unit = rows * lax.rsqrt(jnp.mean(rows * rows, -1, keepdims=True) + EPS)
        N[pl.ds(pl.multiple_of(z * SEQ + g * 16, 16), 16), :] = (unit * GA[0]).astype(BF16)

    def half_rows(ref, zz, half):
        return ref.at[pl.ds(pl.multiple_of(zz * SEQ + half * 32, 32), 32)]

    def ring_z1(name, ref):
        block = ref.at[my_rows(z)]
        send(None, (name + "r", block, block, {"dp": at_zr}), (name + "l", block, block, {"dp": at_zl}))

    def ring_z2(name, ref):
        recv(None, (name + "r", ref.at[my_rows(zl)]))
        a = half_rows(ref, zl, 0)
        send(None, (name + "R", a, a, {"dp": at_zr}))
        recv(None, (name + "l", ref.at[my_rows(zr)]))
        b = half_rows(ref, zr, 1)
        send(None, (name + "L", b, b, {"dp": at_zl}))

    def ring_z3(name, ref):
        recv(None, (name + "R", half_rows(ref, zo, 0)), (name + "L", half_rows(ref, zo, 1)))

    ring_z1("n", N)

    order = (z, zl, zr, zo)
    for n, far in ((1, 1), (2, 3), (3, 2)):
        zz = order[n]
        recv(is0, (f"a2a{far}0", W.at[y, zz, :, pl.ds(0, QW)]),
             (f"a2a{far}1", W.at[y, zz, :, pl.ds(QW, HS)]),
             (f"a2a{far}2", W.at[y, zz, :, pl.ds(QW + HS, HS)]))
        w_out_step(zz, n)
    b_half = lambda yy, half: WKV1.at[yy, z, pl.ds(128 + 64 * half, 64)]
    recv(is1, ("byr", WKV1.at[yl, z, HI]))
    send(is1, ("byR", b_half(yl, 0), b_half(yl, 0), {"dp": at_yr}))
    recv(is1, ("byl", WKV1.at[yr, z, HI]))
    send(is1, ("byL", b_half(yr, 1), b_half(yr, 1), {"dp": at_yl}))
    ring_z2("n", N)
    a_own = WKV1.at[y, z, LO]
    send(is1, ("azr", a_own, a_own, {"dp": at_zr}), ("azl", a_own, a_own, {"dp": at_zl}))
    recv(is1, ("byR", b_half(yo, 0)), ("byL", b_half(yo, 1)))
    b_item = lambda zz: WKV1.at[:, zz, HI]
    send(is1, ("bzr", b_item(z), b_item(z), {"dp": at_zr}), ("bzl", b_item(z), b_item(z), {"dp": at_zl}),
         ("bc", b_item(z), b_item(z), {"section": 0}))

    for side, yy, fwd, at, kept in (("r", yl, "R", at_yr, (0, 2)), ("l", yr, "L", at_yl, (1, 3))):
        for n in range(RING):
            chunk = W.at[yy, order[n]]
            recv(is0, (f"w{n}{side}", chunk))
            if n in kept:
                send(is0, (f"w{n}{fwd}", chunk, chunk, {"dp": at}))
            send(is0, (f"w{n}c{side}", chunk, chunk, {"section": 1}))
    mine = wo_rows(y)
    send(is0,
         ("wo_r", mine, mine, {"dp": at_yr}),
         ("wo_l", mine, mine, {"dp": at_yl}),
         ("wo_c", mine, mine, {"section": 1}))

    a_half = lambda zz, half: WKV1.at[y, zz, pl.ds(64 * half, 64)]
    recv(is1, ("azr", WKV1.at[y, zl, LO]))
    send(is1, ("azR", a_half(zl, 0), a_half(zl, 0), {"dp": at_zr}))
    recv(is1, ("azl", WKV1.at[y, zr, LO]))
    send(is1, ("azL", a_half(zr, 1), a_half(zr, 1), {"dp": at_zl}))

    QA[...] = jnp.zeros_like(QA)

    def project(yy):
        @pl.loop(0, RING)
        def _(zz):
            block = N[:, pl.ds(pl.multiple_of((zz * RING + yy) * BLK, BLK), BLK)]
            QA[...] += mm(block, W[yy, zz])

    def w_core(tag, yy):
        recv(is1, *[(f"w{n}c{tag}", W.at[yy, order[n]]) for n in range(RING)])

    ring_z3("n", N)
    w_core("", y)
    project(y)
    w_core("r", yl)
    project(yl)
    w_core("l", yr)
    project(yr)
    b_two = lambda zz, half: WKV1.at[pl.ds(2 * half, 2), zz, HI]
    recv(is1, ("bzr", b_item(zl)))
    send(is1, ("bzR", b_two(zl, 0), b_two(zl, 0), {"dp": at_zr}),
         ("bcr", b_item(zl), b_item(zl), {"section": 0}))
    recv(is1, ("bzl", b_item(zr)))
    send(is1, ("bzL", b_two(zr, 1), b_two(zr, 1), {"dp": at_zl}),
         ("bcl", b_item(zr), b_item(zr), {"section": 0}))
    for n, fwd in ((0, "R"), (1, "L"), (2, "R"), (3, "L")):
        chunk = W.at[yo, order[n]]
        recv(is0, (f"w{n}{fwd}", chunk))
        send(is0, (f"w{n}co", chunk, chunk, {"section": 1}))

    def wo_half(yy, half):
        return WO.at[pl.ds(pl.multiple_of(yy * HS + half * 64, 64), 64)]

    w_core("o", yo)
    project(yo)
    QB[...] = QA[...].astype(BF16)
    recv(is0, ("wo_r", wo_rows(yl)))
    send(is0, ("wo_R", wo_half(yl, 0), wo_half(yl, 0), {"dp": at_yr}),
         ("wo_cl", wo_rows(yl), wo_rows(yl), {"section": 1}))
    recv(is0, ("wo_l", wo_rows(yr)))
    send(is0, ("wo_L", wo_half(yr, 1), wo_half(yr, 1), {"dp": at_yl}),
         ("wo_cr", wo_rows(yr), wo_rows(yr), {"section": 1}))
    recv(is1, ("azR", a_half(zo, 0)), ("azL", a_half(zo, 1)))
    a_item = lambda yy: WKV1.at[yy, :, LO]

    r_i = lax.broadcasted_iota(jnp.int32, (ROWS, ROWS), 0)
    c_i = lax.broadcasted_iota(jnp.int32, (ROWS, ROWS), 1)
    seen = jnp.logical_and(r_i // SEQ == c_i // SEQ, c_i <= r_i)
    for h in range(GROUP):
        span = slice(h * HS, (h + 1) * HS)
        logits = nt(QB[:, span], QB[:, QW : QW + HS]) * SCALE
        grown = jnp.where(seen, jnp.exp(jnp.where(seen, logits, 0.0)), 0.0)
        weights = grown / jnp.sum(grown, -1, keepdims=True)
        WA[h] = weights
        context = mm(weights.astype(BF16), QB[:, QW + HS :])
        CTX[:, span] = context.astype(BF16)
        CTT[span, :] = context.T.astype(BF16)
    send(None, ("ctt", CTT, CTP, {"section": other}))
    send(is1, ("q1", WQ1, WQ1, {"section": 0}), ("o1", WO1, WO1, {"section": 0}))

    recv(is0, ("wo_R", wo_half(yo, 0)), ("wo_L", wo_half(yo, 1)))
    send(is0, ("wo_co", wo_rows(yo), wo_rows(yo), {"section": 1}))
    recv(is1, ("wo_c", wo_rows(y)), ("wo_cl", wo_rows(yl)), ("wo_cr", wo_rows(yr)), ("wo_co", wo_rows(yo)))
    send(is1, ("ayr", a_item(y), a_item(y), {"dp": at_yr}), ("ayl", a_item(y), a_item(y), {"dp": at_yl}),
         ("ac", a_item(y), a_item(y), {"section": 0}))

    @pl.loop(0, 8)
    def _(t):
        span = pl.ds(pl.multiple_of(t * 512, 512), 512)
        OP[:, span] = mm(CTX[...], WO[:, span]).astype(BF16)

    send(None, ("o1r", half_rows(OP, zo, 0), FWD.at[0], {"dp": at_zr}),
         ("o1l", half_rows(OP, zo, 1), FWD.at[1], {"dp": at_zl}))
    for side, tag, dest, at in ((0, "o1r", zr, at_zr), (1, "o1l", zl, at_zl)):
        recv(None, (tag, FWD.at[side]))

        @pl.loop(0, 2)
        def _(g):
            rows = pl.ds(pl.multiple_of(dest * SEQ + side * 32 + g * 16, 16), 16)
            part = pl.ds(pl.multiple_of(g * 16, 16), 16)
            OP[rows, :] = (OP[rows, :].astype(F32) + FWD[side, part, :].astype(F32)).astype(BF16)

        send(None, (f"o2{side}", OP.at[my_rows(dest)], LAND.at[side], {"dp": at}))

    a_two = lambda yy, half: WKV1.at[yy, pl.ds(2 * half, 2), LO]
    recv(is1, ("bzR", b_two(zo, 0)), ("bzL", b_two(zo, 1)))
    send(is1, ("bco", b_item(zo), b_item(zo), {"section": 0}))
    for tag, yy, fwd, half, at in (("r", yl, "R", 0, at_yr), ("l", yr, "L", 1, at_yl)):
        recv(is1, ("ay" + tag, a_item(yy)))
        send(is1, ("ay" + fwd, a_two(yy, half), a_two(yy, half), {"dp": at}),
             ("ac" + tag, a_item(yy), a_item(yy), {"section": 0}))

    recv(None, ("o20", LAND.at[0]), ("o21", LAND.at[1]))

    length = jnp.where(is0, lens[0, 0], lens[0, 1])
    NL[...] = jnp.zeros_like(NL)
    HL[...] = jnp.zeros_like(HL)

    def last_rows(g):
        return lax.broadcasted_iota(jnp.int32, (16, D), 0) + g * 16 == length - 1

    @pl.loop(0, 4)
    def _(g):
        part = pl.ds(pl.multiple_of(g * 16, 16), 16)
        own = pl.ds(pl.multiple_of(z * SEQ + g * 16, 16), 16)
        total = X[part, :].astype(F32) + (
            OP[own, :].astype(F32) + LAND[0, part, :].astype(F32) + LAND[1, part, :].astype(F32)
        )
        hidden = total.astype(BF16)
        H1[part, :] = hidden
        rows = hidden.astype(F32)
        unit = rows * lax.rsqrt(jnp.mean(rows * rows, -1, keepdims=True) + EPS)
        normed = (unit * GA[1]).astype(BF16)
        N1[part, :] = normed
        last = last_rows(g)
        NL[...] += jnp.sum(jnp.where(last, normed.astype(F32), 0.0), 0, keepdims=True)
        HL[...] += jnp.sum(jnp.where(last, rows, 0.0), 0, keepdims=True)

    for j in range(N_DP):
        S1[j] = NL[:, j * BLK : (j + 1) * BLK]
    exchange("e1", lambda peer, slot: S1.at[peer], R1)
    R1[N_DP - 1] = S1[dp]
    KVA1[...] = jnp.zeros_like(KVA1)

    def project1(yy):
        @pl.loop(0, RING)
        def _(zz):
            block = N1[:, pl.ds(pl.multiple_of((zz * RING + yy) * BLK, BLK), BLK)]
            KVA1[...] += mm(block, WKV1[yy, zz])

    recv(is0, ("q1", WQ1), ("o1", WO1), ("ac", a_item(y)),
         ("bc", b_item(z)), ("bcr", b_item(zl)), ("bcl", b_item(zr)), ("bco", b_item(zo)))
    project1(y)
    landed("e1", R1)
    for j in range(N_DP):
        X1[j : j + 1, :] = R1[j]
    back = mm(X1[...].astype(BF16), WQ1[...])
    for j in range(N_DP):
        T2[j] = back[j : j + 1, :]
    exchange("e2", lambda peer, slot: T2.at[slot], R2)
    R2[N_DP - 1] = T2[N_DP - 1]
    for tag, yy in (("r", yl), ("l", yr)):
        recv(is0, ("ac" + tag, a_item(yy)))
        project1(yy)
    recv(is1, ("ayR", a_two(yo, 0)), ("ayL", a_two(yo, 1)))
    send(is1, ("aco", a_item(yo), a_item(yo), {"section": 0}))
    recv(is0, ("aco", a_item(yo)))
    project1(yo)
    for g in range(RING):
        KC[g * SEQ : (g + 1) * SEQ, :] = KVA1[:, g * HS : (g + 1) * HS].astype(BF16)
        VC[g * SEQ : (g + 1) * SEQ, :] = KVA1[:, (RING + g) * HS : (RING + g + 1) * HS].astype(BF16)
    landed("e2", R2)
    q_row = R2[0]
    for j in range(1, N_DP):
        q_row = q_row + R2[j]
    for h in range(HEADS):
        Q16[h : h + 1, :] = q_row[:, h * HS : (h + 1) * HS]
    q_last = Q16[...].astype(BF16)

    h_i = lax.broadcasted_iota(jnp.int32, (HEADS, RING * SEQ), 0)
    k_i = lax.broadcasted_iota(jnp.int32, (HEADS, RING * SEQ), 1)
    seen1 = jnp.logical_and(h_i // GROUP == k_i // SEQ, k_i % SEQ < length)
    logits = nt(q_last, KC[...]) * SCALE
    grown = jnp.where(seen1, jnp.exp(jnp.where(seen1, logits, 0.0)), 0.0)
    weights1 = grown / jnp.sum(grown, -1, keepdims=True)
    probs1 = weights1.astype(BF16)
    context1 = mm(probs1, VC[...]).astype(BF16).astype(F32)
    for h in range(HEADS):
        S3[h] = context1[h : h + 1, :]
    exchange("e3", lambda peer, slot: S3.at[peer], R3)
    R3[N_DP - 1] = S3[dp]
    landed("e3", R3)
    for j in range(N_DP):
        X3[j : j + 1, :] = R3[j]
    x3 = X3[...].astype(BF16)
    for t in range(4):
        back = mm(x3, WO1[:, t * 1024 : (t + 1) * 1024])
        for j in range(N_DP):
            T4[j, :, t * 1024 : (t + 1) * 1024] = back[j : j + 1, :]
    exchange("e4", lambda peer, slot: T4.at[slot], R4)
    R4[N_DP - 1] = T4[N_DP - 1]
    landed("e4", R4)
    update = R4[0]
    for j in range(1, N_DP):
        update = update + R4[j]
    final = (HL[...] + update).astype(BF16).astype(F32)

    scale1 = lax.rsqrt(jnp.mean(final * final, -1, keepdims=True) + EPS)
    unit1 = final * scale1
    weighed = unit1 * HD[...]
    score = jnp.sum(weighed, -1, keepdims=True)
    mine_sc = m * 2 + s
    SCB[mine_sc] = jnp.broadcast_to(score, (1, HS))
    send(None, *[
        (f"sc{dm}{ds}", SCB.at[mine_sc], SCB.at[mine_sc], {"member": (m + dm) % 4, "section": (s + ds) % 2})
        for dm in range(4) for ds in range(2) if dm or ds
    ])
    toward = scale1 * (HD[...] - unit1 * (score / D))
    S6[...] = toward.astype(BF16).astype(F32)
    exchange("e6", lambda peer, slot: S6, R6)
    R6[N_DP - 1] = S6[...]
    recv(None, *[
        (f"sc{dm}{ds}", SCB.at[((m + 4 - dm) % 4) * 2 + (s + ds) % 2])
        for dm in range(4) for ds in range(2) if dm or ds
    ])
    chosen = (SCB[0] + SCB[2] + SCB[4] + SCB[6]) / 4
    rejected = (SCB[1] + SCB[3] + SCB[5] + SCB[7]) / 4
    spread = jax.nn.sigmoid(rejected - chosen)
    direction = jnp.where(is0, -spread, spread)
    landed("e6", R6)
    for j in range(N_DP):
        X6[j : j + 1, :] = R6[j]
    back = jnp.zeros((N_DP, HS), F32)
    for t in range(4):
        span = slice(t * 1024, (t + 1) * 1024)
        back = back + nt(X6[:, span].astype(BF16), WO1[:, span])
    for j in range(N_DP):
        T7[j] = back[j : j + 1, :]
    exchange("e7", lambda peer, slot: T7.at[slot], R7)
    R7[N_DP - 1] = T7[N_DP - 1]
    landed("e7", R7)
    for h in range(HEADS):
        DC[h : h + 1, :] = R7[slot_of(h)]
    d_ctx = (DC[...] * direction).astype(BF16)
    d_probs = nt(d_ctx, VC[...])
    leaned = weights1 * d_probs
    d_logits = (leaned - weights1 * jnp.sum(leaned, -1, keepdims=True)) * SCALE
    d_logits = d_logits.astype(BF16)
    d_query = mm(d_logits, KC[...]).astype(BF16).astype(F32)
    for h in range(HEADS):
        S8[:, h * HS : (h + 1) * HS] = d_query[h : h + 1, :]
    lane = lax.broadcasted_iota(jnp.int32, (1, HS), 1)
    meta = jnp.where(lane == 0, direction, jnp.where(lane == 1, chosen, rejected))
    S8[:, HEADS * HS :] = jnp.where(lane == 3, route[0].astype(F32), meta)
    exchange("e8", lambda peer, slot: S8, R8)
    R8[N_DP - 1] = S8[...]
    d_key = tn(d_logits, q_last)
    d_value = tn(probs1, d_ctx)
    for g in range(RING):
        DKV[:, g * HS : (g + 1) * HS] = d_key[g * SEQ : (g + 1) * SEQ, :].astype(BF16)
        DKV[:, (RING + g) * HS : (RING + g + 1) * HS] = d_value[g * SEQ : (g + 1) * SEQ, :].astype(BF16)

    @pl.loop(0, N_DP)
    def _(j):
        span = pl.ds(pl.multiple_of(j * BLK, BLK), BLK)
        GN[:, span] = nt(DKV[...], WKV1[j % RING, j // RING])

    landed("e8", R8)
    for j in range(N_DP):
        X8[j : j + 1, :] = R8[j, :, : HEADS * HS]
    back = nt(X8[...].astype(BF16), WQ1[...])
    for j in range(N_DP):
        T9[j] = back[j : j + 1, :]
    exchange("e9", lambda peer, slot: T9.at[slot], R9)
    R9[N_DP - 1] = T9[N_DP - 1]
    answer = jnp.zeros((1, HS), F32)
    for j in range(N_DP):
        extra = R8[j, :, HEADS * HS :]
        answer = answer + jnp.where(extra[:, 3:4] == dp.astype(F32), extra, 0.0)
        GC[s, j : j + 1, :] = R6[j] * extra[:, 0:1]
    scores_out[...] = answer[:, 1:3]
    XC[s] = X3[...]
    send(is0, ("xc", XC.at[0], XC.at[0], {"section": 1}), ("gc", GC.at[0], GC.at[0], {"section": 1}))
    landed("e9", R9)
    for h in range(N_DP):
        GNL[:, h * BLK : (h + 1) * BLK] = R9[slot_of(h)]

    HL[...] = (toward * direction[:, 0:1]).astype(BF16).astype(F32)
    NL[...] = jnp.zeros_like(NL)

    @pl.loop(0, 4)
    def _(g):
        part = pl.ds(pl.multiple_of(g * 16, 16), 16)
        rows = H1[part, :].astype(F32)
        scale = lax.rsqrt(jnp.mean(rows * rows, -1, keepdims=True) + EPS)
        unit = rows * scale
        last = last_rows(g)
        d_normed = GN[part, :] + jnp.where(last, GNL[...], 0.0)
        NL[...] += jnp.sum(d_normed * unit, 0, keepdims=True)
        pulled = d_normed * GA[1]
        d_rows = scale * (pulled - unit * jnp.mean(pulled * unit, -1, keepdims=True))
        d_rows = (d_rows + jnp.where(last, HL[...], 0.0)).astype(BF16)
        own = pl.ds(pl.multiple_of(z * SEQ + g * 16, 16), 16)
        for c in range(2):
            for half in range(2):
                first = half * HALF + c * QUART
                G[c, own, half * QUART : (half + 1) * QUART] = d_rows[:, first : first + QUART]

    across = pl.ds(pl.multiple_of(other * QUART, QUART), QUART)

    def to_core(c, n, zz):
        send(None, (f"gp{c}{n}", G.at[c, my_rows(zz), across], GP.at[c, my_rows(zz)], {"section": other}))

    for c in range(2):
        ring_z1(f"g{c}", G.at[c])
    for c in range(2):
        to_core(c, 0, z)

    recv(is1, ("xc", XC.at[0]), ("gc", GC.at[0]))

    @pl.when(is1)
    def _():
        rows_a, rows_b = XC[0].astype(BF16), XC[1].astype(BF16)

        @pl.loop(0, 8)
        def _(t):
            span = pl.ds(pl.multiple_of(t * 512, 512), 512)
            grad_out[0, 0, :, span] = (
                tn(rows_a, GC[0, :, span].astype(BF16)) + tn(rows_b, GC[1, :, span].astype(BF16))
            ).astype(BF16)

    for h in range(N_DP):
        SG[h, :, BLK:] = NL[:, h * BLK : (h + 1) * BLK]

    for c in range(2):
        ring_z2(f"g{c}", G.at[c])
        to_core(c, 1, zl)
        to_core(c, 2, zr)

    recv(None, ("ctt", CTP))

    def head_rows(c, yy):
        return GOP.at[c, pl.ds(pl.multiple_of(yy * HS, HS), HS)]

    def head_half(c, yy, half):
        return GOP.at[c, pl.ds(pl.multiple_of(yy * HS + half * 64, 64), 64)]

    def scatter1(c):
        ring_z3(f"g{c}", G.at[c])
        to_core(c, 3, zo)
        recv(None, *[(f"gp{c}{n}", GP.at[c, my_rows(zz)]) for n, zz in enumerate((z, zl, zr, zo))])

        @pl.loop(0, 2)
        def _(u):
            span = pl.ds(pl.multiple_of(u * 512, 512), 512)
            here = pl.ds(pl.multiple_of(s * QUART + u * 512, 512), 512)
            GOP[c, :, span] = (mm(CTT[...], G[c, :, here]) + mm(CTP[...], GP[c, :, span])).astype(BF16)

        send(None, (f"r1r{c}", head_half(c, yo, 0), FWD2.at[c, 0], {"dp": at_yr}),
             (f"r1l{c}", head_half(c, yo, 1), FWD2.at[c, 1], {"dp": at_yl}))
        send(is1, (f"rc{c}", head_rows(c, y), LAND2.at[c, 4], {"section": 0}))

    def scatter2(c):
        for side, tag, dest, at in ((0, "r1r", yr, at_yr), (1, "r1l", yl, at_yl)):
            recv(None, (f"{tag}{c}", FWD2.at[c, side]))
            rows = pl.ds(pl.multiple_of(dest * HS + side * 64, 64), 64)
            GOP[c, rows, :] = (GOP[c, rows, :].astype(F32) + FWD2[c, side].astype(F32)).astype(BF16)
            send(is0, (f"ra{side}{c}", head_rows(c, dest), LAND2.at[c, side], {"dp": at, "section": 0}))
            send(is1, (f"rb{side}{c}", head_rows(c, dest), LAND2.at[c, 2 + side], {"dp": at, "section": 0}))

    scatter1(0)
    scatter1(1)
    scatter2(0)

    DCT[...] = jnp.zeros_like(DCT)

    @pl.loop(0, 8)
    def _(t):
        c, u = t // RING, t % RING
        span = pl.ds(pl.multiple_of(u * 512, 512), 512)
        here = pl.ds(pl.multiple_of((u // 2) * HALF + c * QUART + (u % 2) * 512, 512), 512)
        DCT[...] += nt(G[c, :, span], WO[:, here])

    scatter2(1)

    d_key = jnp.zeros((ROWS, HS), F32)
    d_value = jnp.zeros((ROWS, HS), F32)
    for h in range(GROUP):
        span = slice(h * HS, (h + 1) * HS)
        d_ctx = DCT[:, span].astype(BF16)
        weights = WA[h]
        leaned = weights * nt(d_ctx, QB[:, QW + HS :])
        d_logits = (leaned - weights * jnp.sum(leaned, -1, keepdims=True)) * SCALE
        d_logits = d_logits.astype(BF16)
        DQB[:, span] = mm(d_logits, QB[:, QW : QW + HS]).astype(BF16)
        d_key = d_key + tn(d_logits, QB[:, span])
        d_value = d_value + tn(weights.astype(BF16), d_ctx)
    DQB[:, QW : QW + HS] = d_key.astype(BF16)
    DQB[:, QW + HS :] = d_value.astype(BF16)

    @pl.loop(0, N_DP)
    def _(j):
        span = pl.ds(pl.multiple_of(j * BLK, BLK), BLK)
        yy, zz = j % RING, j // RING
        d_normed = nt(DQB[...], W[yy, zz])
        sums = jnp.sum(d_normed * N[:, span].astype(F32), 0, keepdims=True)
        SG[j, :, :BLK] = sums / GA[0, :, span]

    exchange("e10", lambda peer, slot: SG.at[peer], RG)
    RG[N_DP - 1] = SG[dp]
    landed("e10", RG)
    total = RG[0]
    for j in range(1, N_DP):
        total = total + RG[j]
    SP[...] = total
    send(None, ("sp", SP, PG, {"section": other}))

    recv(None, ("sp", PG))
    both = total + PG[...]
    gain_out[0] = jnp.where(is0, both[:, :BLK], both[:, BLK:])

    for c in range(2):
        recv(is0, (f"rc{c}", LAND2.at[c, 4]), *[
            (f"r{kind}{side}{c}", LAND2.at[c, 2 * n + side]) for n, kind in enumerate("ab") for side in range(2)
        ])

    @pl.when(is0)
    def _():
        @pl.loop(0, 8)
        def _(g):
            part = pl.ds(pl.multiple_of(g * 16, 16), 16)
            own = pl.ds(pl.multiple_of(y * HS + g * 16, 16), 16)
            for c in range(2):
                grad_out[0, 0, part, c * QUART : (c + 1) * QUART] = (GOP[c, own, :].astype(F32) + (
                    LAND2[c, 0, part, :].astype(F32) + LAND2[c, 1, part, :].astype(F32)
                )).astype(BF16)
                grad_out[0, 0, part, HALF + c * QUART : HALF + (c + 1) * QUART] = (LAND2[c, 4, part, :].astype(F32) + (
                    LAND2[c, 2, part, :].astype(F32) + LAND2[c, 3, part, :].astype(F32)
                )).astype(BF16)

    for cond, fin in pending:
        guarded(cond, fin)
    assert len(ids) <= N_SEMS, len(ids)


def body(embeds, lengths, route, w_query, w_keyval, w_out, norm_gain, head):
    hbm = pl.BlockSpec(memory_space=pl.ANY)
    vmem = pl.BlockSpec(memory_space=pltpu.VMEM)
    smem = pl.BlockSpec(memory_space=pltpu.SMEM)
    V = pltpu.VMEM
    row = lambda n: V((1, n), F32)
    slots = lambda n: V((N_DP, 1, n), F32)
    scratch = [
        V((SEQ, D), BF16), V((2, 1, D), F32), row(D), V((ROWS, D), BF16),
        V((RING, RING, BLK, QW + 2 * HS), BF16), V((QW, D), BF16),
        V((BLK, HEADS * HS), BF16), V((HS, D), BF16), V((RING, RING, BLK, 2 * RING * HS), BF16),
        V((ROWS, QW + 2 * HS), F32), V((ROWS, QW + 2 * HS), BF16),
        V((GROUP, ROWS, ROWS), F32), V((ROWS, QW), BF16), V((QW, ROWS), BF16), V((QW, ROWS), BF16),
        V((ROWS, D), BF16), V((2, 32, D), BF16), V((2, SEQ, D), BF16),
        V((SEQ, D), BF16), V((SEQ, D), BF16), V((SEQ, 2 * RING * HS), F32),
        V((RING * SEQ, HS), BF16), V((RING * SEQ, HS), BF16), V((HEADS, HS), F32),
        row(D), row(D), slots(BLK), slots(BLK), V((N_DP, BLK), F32), slots(HEADS * HS), slots(HEADS * HS),
        slots(HS), slots(HS), V((N_DP, HS), F32), slots(D), slots(D), V((8, 1, HS), F32),
        row(D), slots(D), V((N_DP, D), F32), slots(HS), slots(HS), V((HEADS, HS), F32),
        row(HEADS * HS + HS), slots(HEADS * HS + HS), V((N_DP, HEADS * HS), F32), slots(BLK), slots(BLK),
        row(D), V((2, N_DP, HS), F32), V((2, N_DP, D), F32), V((SEQ, D), F32), V((SEQ, 2 * RING * HS), BF16),
        V((2, ROWS, HALF), BF16), V((2, ROWS, QUART), BF16), V((ROWS, QW), F32), V((ROWS, QW + 2 * HS), BF16),
        V((2, QW, QUART), BF16), V((2, 2, 64, QUART), BF16), V((2, 5, HS, QUART), BF16),
        slots(2 * BLK), slots(2 * BLK), row(2 * BLK), row(2 * BLK),
        pltpu.SemaphoreType.DMA((N_SEMS,)), pltpu.SemaphoreType.DMA((N_SEMS,)), pltpu.SemaphoreType.DMA((8,)),
    ]
    scores, grad, gains = pl.pallas_call(
        kernel,
        out_shape=(
            jax.ShapeDtypeStruct((1, 2), F32),
            jax.ShapeDtypeStruct((1, 1, HS, D), BF16),
            jax.ShapeDtypeStruct((1, 1, BLK), F32),
        ),
        in_specs=[hbm, smem, smem, hbm, hbm, hbm, hbm, hbm],
        out_specs=(vmem, vmem, vmem),
        scratch_shapes=scratch,
        compiler_params=pltpu.CompilerParams(
            collective_id=0, has_side_effects=True, vmem_limit_bytes=60 * 1024 * 1024
        ),
    )(embeds, lengths, route, w_query, w_keyval, w_out, norm_gain, head)
    return scores, grad.astype(F32), gains


def solution(mesh):
    placed = (
        P("member", "dp", None, None, None),
        P("dp", None),
        P("dp"),
        P("member", "section", "dp", None),
        P("member", "section", "dp", None),
        P("member", "section", "dp", None),
        P("member", "section", None),
        P("member", None),
    )
    return jax.shard_map(
        body,
        mesh=mesh,
        in_specs=placed,
        out_specs=(P("dp", None), P("member", "section", "dp", None), P("member", "section", "dp")),
        check_vma=False,
    )
```

```python
import jax
import jax.numpy as jnp
from jax import lax
from jax.experimental import pallas as pl
from jax.experimental.pallas import tpu as pltpu
from jax.sharding import PartitionSpec as P

MESH = pl.DeviceIdType.MESH
F32 = jnp.float32
BF16 = jnp.bfloat16
EPS = 1e-05
HS = 128
SEQ = 64
D = 4096
RING = 4
N_DP = RING * RING
HEADS = 16
GROUP = HEADS // RING
QW = GROUP * HS
ROWS = RING * SEQ
BLK = D // N_DP
HALF = D // 2
QUART = D // 4
SCALE = HS ** (-0.5)
N_SEMS = 160


def mm(a, b):
    return jnp.dot(a, b, preferred_element_type=F32)


def nt(a, b):
    return lax.dot_general(a, b, (((1,), (1,)), ((), ())), preferred_element_type=F32)


def tn(a, b):
    return lax.dot_general(a, b, (((0,), (0,)), ((), ())), preferred_element_type=F32)


def kernel(
    emb, lens, route, wq, wkv, wo, gain, head,
    scores_out, grad_out, gain_out,
    X, GA, HD, N, W, WO, WQ1, WO1, WKV1,
    QA, QB, WA, CTX, CTT, CTP, OP, FWD, LAND,
    H1, N1, KVA1, KC, VC, Q16,
    NL, HL, S1, R1, X1, T2, R2, S3, R3, X3, T4, R4, SCB, S6, R6, X6, T7, R7, DC,
    S8, R8, X8, T9, R9, GNL, XC, GC, GN, DKV,
    G, GP, DCT, DQB, GOP, FWD2, LAND2, SG, RG, SP, PG,
    ssem, rsem, lsem,
):
    s = lax.axis_index("section")
    m = lax.axis_index("member")
    dp = lax.axis_index("dp")
    z = dp // RING
    y = dp % RING
    other = 1 - s
    zr, zl, zo = (z + 1) % RING, (z + 3) % RING, (z + 2) % RING
    yr, yl, yo = (y + 1) % RING, (y + 3) % RING, (y + 2) % RING
    at_zr, at_zl, at_zo = zr * RING + y, zl * RING + y, zo * RING + y
    at_yr, at_yl = z * RING + yr, z * RING + yl
    is0 = s == 0
    is1 = s == 1
    ids = {}
    pending = []

    def desc(name, src, dst, **dev):
        i = ids.setdefault(name, len(ids))
        return pltpu.make_async_remote_copy(
            src_ref=src, dst_ref=dst, send_sem=ssem.at[i], recv_sem=rsem.at[i],
            device_id=dev, device_id_type=MESH,
        )

    def guarded(cond, act):
        if cond is None:
            act()
        else:
            pl.when(cond)(act)

    def send(cond, *items):
        copies = [desc(name, src, dst, **dev) for name, src, dst, dev in items]

        def act():
            for c in copies:
                c.start()

        guarded(cond, act)

        def fin():
            for c in copies:
                c.wait_send()

        pending.append((cond, fin))

    def recv(cond, *items):
        copies = [desc(name, dst, dst, section=other) for name, dst in items]

        def act():
            for c in copies:
                c.wait_recv()

        guarded(cond, act)

    def exchange(name, src_of, land):
        i = ids.setdefault(name, len(ids))

        @pl.loop(1, N_DP)
        def _(k):
            peer = (dp + k) % N_DP
            pltpu.make_async_remote_copy(
                src_ref=src_of(peer, N_DP - 1 - k), dst_ref=land.at[k - 1],
                send_sem=ssem.at[i], recv_sem=rsem.at[i],
                device_id={"dp": peer}, device_id_type=MESH,
            ).start()

        whole = desc(name, land.at[pl.ds(0, N_DP - 1)], land.at[pl.ds(0, N_DP - 1)], section=other)
        pending.append((None, whole.wait_send))

    def landed(name, land):
        desc(name, land.at[pl.ds(0, N_DP - 1)], land.at[pl.ds(0, N_DP - 1)], section=other).wait_recv()

    def slot_of(h):
        return (dp + N_DP - 1 - h) % N_DP

    lx = pltpu.make_async_copy(emb.at[0, 0, s], X, lsem.at[0])
    lg = pltpu.make_async_copy(gain.at[0], GA.at[s], lsem.at[1])
    lh = pltpu.make_async_copy(head, HD, lsem.at[2])
    lx.start()
    lg.start()
    lh.start()
    wq_mine, wkv_mine, wo_mine = wq.at[0, 0], wkv.at[0, 0], wo.at[0, 0]

    def cols(ref, first, size):
        return ref.at[:, pl.ds(pl.multiple_of(first, HS), size)]

    def slices(dest_z):
        return (
            (cols(wq_mine, dest_z * QW, QW), W.at[y, z, :, pl.ds(0, QW)]),
            (cols(wkv_mine, dest_z * HS, HS), W.at[y, z, :, pl.ds(QW, HS)]),
            (cols(wkv_mine, RING * HS + dest_z * HS, HS), W.at[y, z, :, pl.ds(QW + HS, HS)]),
        )

    wo_rows = lambda yy: WO.at[pl.ds(pl.multiple_of(yy * HS, HS), HS)]
    local0 = [pltpu.make_async_copy(a, b, lsem.at[3 + n]) for n, (a, b) in enumerate(slices(z))]
    local0.append(pltpu.make_async_copy(wo_mine, wo_rows(y), lsem.at[6]))
    local1 = [
        pltpu.make_async_copy(wq_mine, WQ1, lsem.at[3]),
        pltpu.make_async_copy(wkv_mine, WKV1.at[y, z], lsem.at[4]),
        pltpu.make_async_copy(wo_mine, WO1, lsem.at[5]),
    ]

    @pl.when(is0)
    def _():
        for c in local0:
            c.start()

    @pl.when(is1)
    def _():
        for c in local1:
            c.start()

    barrier = pltpu.get_barrier_semaphore()

    @pl.loop(1, N_DP)
    def _(k):
        pl.semaphore_signal(barrier, inc=1, device_id={"dp": (dp + k) % N_DP}, device_id_type=MESH)

    for dm in range(4):
        for ds in range(2):
            if dm or ds:
                pl.semaphore_signal(
                    barrier, inc=1, device_id={"member": (m + dm) % 4, "section": (s + ds) % 2},
                    device_id_type=MESH,
                )
    for at in (at_yr, at_yl):
        pl.semaphore_signal(barrier, inc=1, device_id={"section": other, "dp": at}, device_id_type=MESH)
    pl.semaphore_wait(barrier, N_DP - 1 + 7 + 2)

    for far, at in ((1, at_zr), (3, at_zl), (2, at_zo)):
        dest = (z + far) % RING
        send(is0, *[(f"a2a{far}{n}", a, b, {"dp": at}) for n, (a, b) in enumerate(slices(dest))])

    def w_out_step(zz, n):
        chunk = W.at[y, zz]
        send(is0, (f"w{n}r", chunk, chunk, {"dp": at_yr}), (f"w{n}l", chunk, chunk, {"dp": at_yl}),
             (f"w{n}c", chunk, chunk, {"section": 1}))

    @pl.when(is0)
    def _():
        for c in local0:
            c.wait()

    @pl.when(is1)
    def _():
        for c in local1:
            c.wait()

    w_out_step(z, 0)
    LO, HI = pl.ds(0, 128), pl.ds(128, 128)
    b_own = WKV1.at[y, z, HI]
    send(is1, ("byr", b_own, b_own, {"dp": at_yr}), ("byl", b_own, b_own, {"dp": at_yl}))
    send(None, ("gain", gain.at[0], GA.at[s], {"section": other}))

    lx.wait()
    lg.wait()
    lh.wait()
    recv(None, ("gain", GA.at[other]))
    my_rows = lambda zz: pl.ds(pl.multiple_of(zz * SEQ, SEQ), SEQ)

    @pl.loop(0, 4)
    def _(g):
        part = pl.ds(pl.multiple_of(g * 16, 16), 16)
        rows = X[part, :].astype(F32)
        unit = rows * lax.rsqrt(jnp.mean(rows * rows, -1, keepdims=True) + EPS)
        N[pl.ds(pl.multiple_of(z * SEQ + g * 16, 16), 16), :] = (unit * GA[0]).astype(BF16)

    def half_rows(ref, zz, half):
        return ref.at[pl.ds(pl.multiple_of(zz * SEQ + half * 32, 32), 32)]

    def ring_z1(name, ref):
        block = ref.at[my_rows(z)]
        send(None, (name + "r", block, block, {"dp": at_zr}), (name + "l", block, block, {"dp": at_zl}))

    def ring_z2(name, ref):
        recv(None, (name + "r", ref.at[my_rows(zl)]))
        a = half_rows(ref, zl, 0)
        send(None, (name + "R", a, a, {"dp": at_zr}))
        recv(None, (name + "l", ref.at[my_rows(zr)]))
        b = half_rows(ref, zr, 1)
        send(None, (name + "L", b, b, {"dp": at_zl}))

    def ring_z3(name, ref):
        recv(None, (name + "R", half_rows(ref, zo, 0)), (name + "L", half_rows(ref, zo, 1)))

    ring_z1("n", N)

    order = (z, zl, zr, zo)
    for n, far in ((1, 1), (2, 3), (3, 2)):
        zz = order[n]
        recv(is0, (f"a2a{far}0", W.at[y, zz, :, pl.ds(0, QW)]),
             (f"a2a{far}1", W.at[y, zz, :, pl.ds(QW, HS)]),
             (f"a2a{far}2", W.at[y, zz, :, pl.ds(QW + HS, HS)]))
        w_out_step(zz, n)
    b_half = lambda yy, half: WKV1.at[yy, z, pl.ds(128 + 64 * half, 64)]
    recv(is1, ("byr", WKV1.at[yl, z, HI]))
    send(is1, ("byR", b_half(yl, 0), b_half(yl, 0), {"dp": at_yr}))
    recv(is1, ("byl", WKV1.at[yr, z, HI]))
    send(is1, ("byL", b_half(yr, 1), b_half(yr, 1), {"dp": at_yl}))
    for side, yy, fwd, at, kept in (("r", yl, "R", at_yr, (0, 2)), ("l", yr, "L", at_yl, (1, 3))):
        for n in range(RING):
            chunk = W.at[yy, order[n]]
            recv(is0, (f"w{n}{side}", chunk))
            if n in kept:
                send(is0, (f"w{n}{fwd}", chunk, chunk, {"dp": at}))
            send(is0, (f"w{n}c{side}", chunk, chunk, {"section": 1}))
    mine = wo_rows(y)
    send(is0,
         ("wo_r", mine, mine, {"dp": at_yr}),
         ("wo_l", mine, mine, {"dp": at_yl}),
         ("wo_c", mine, mine, {"section": 1}))

    ring_z2("n", N)
    a_own = WKV1.at[y, z, LO]
    send(is1, ("azr", a_own, a_own, {"dp": at_zr}), ("azl", a_own, a_own, {"dp": at_zl}))
    recv(is1, ("byR", b_half(yo, 0)), ("byL", b_half(yo, 1)))
    b_item = lambda zz: WKV1.at[:, zz, HI]
    send(is1, ("bzr", b_item(z), b_item(z), {"dp": at_zr}), ("bzl", b_item(z), b_item(z), {"dp": at_zl}),
         ("bc", b_item(z), b_item(z), {"section": 0}))

    a_half = lambda zz, half: WKV1.at[y, zz, pl.ds(64 * half, 64)]
    recv(is1, ("azr", WKV1.at[y, zl, LO]))
    send(is1, ("azR", a_half(zl, 0), a_half(zl, 0), {"dp": at_zr}))
    recv(is1, ("azl", WKV1.at[y, zr, LO]))
    send(is1, ("azL", a_half(zr, 1), a_half(zr, 1), {"dp": at_zl}))

    QA[...] = jnp.zeros_like(QA)

    def project(yy):
        @pl.loop(0, RING)
        def _(zz):
            block = N[:, pl.ds(pl.multiple_of((zz * RING + yy) * BLK, BLK), BLK)]
            QA[...] += mm(block, W[yy, zz])

    def w_core(tag, yy):
        recv(is1, *[(f"w{n}c{tag}", W.at[yy, order[n]]) for n in range(RING)])

    ring_z3("n", N)
    w_core("", y)
    project(y)
    w_core("r", yl)
    project(yl)
    w_core("l", yr)
    project(yr)
    b_two = lambda zz, half: WKV1.at[pl.ds(2 * half, 2), zz, HI]
    recv(is1, ("bzr", b_item(zl)))
    send(is1, ("bzR", b_two(zl, 0), b_two(zl, 0), {"dp": at_zr}),
         ("bcr", b_item(zl), b_item(zl), {"section": 0}))
    recv(is1, ("bzl", b_item(zr)))
    send(is1, ("bzL", b_two(zr, 1), b_two(zr, 1), {"dp": at_zl}),
         ("bcl", b_item(zr), b_item(zr), {"section": 0}))
    for n, fwd in ((0, "R"), (1, "L"), (2, "R"), (3, "L")):
        chunk = W.at[yo, order[n]]
        recv(is0, (f"w{n}{fwd}", chunk))
        send(is0, (f"w{n}co", chunk, chunk, {"section": 1}))

    def wo_half(yy, half):
        return WO.at[pl.ds(pl.multiple_of(yy * HS + half * 64, 64), 64)]

    w_core("o", yo)
    project(yo)
    QB[...] = QA[...].astype(BF16)
    recv(is0, ("wo_r", wo_rows(yl)))
    send(is0, ("wo_R", wo_half(yl, 0), wo_half(yl, 0), {"dp": at_yr}),
         ("wo_cl", wo_rows(yl), wo_rows(yl), {"section": 1}))
    recv(is0, ("wo_l", wo_rows(yr)))
    send(is0, ("wo_L", wo_half(yr, 1), wo_half(yr, 1), {"dp": at_yl}),
         ("wo_cr", wo_rows(yr), wo_rows(yr), {"section": 1}))
    recv(is1, ("azR", a_half(zo, 0)), ("azL", a_half(zo, 1)))
    a_item = lambda yy: WKV1.at[yy, :, LO]

    r_i = lax.broadcasted_iota(jnp.int32, (ROWS, ROWS), 0)
    c_i = lax.broadcasted_iota(jnp.int32, (ROWS, ROWS), 1)
    seen = jnp.logical_and(r_i // SEQ == c_i // SEQ, c_i <= r_i)
    for h in range(GROUP):
        span = slice(h * HS, (h + 1) * HS)
        logits = nt(QB[:, span], QB[:, QW : QW + HS]) * SCALE
        grown = jnp.where(seen, jnp.exp(jnp.where(seen, logits, 0.0)), 0.0)
        weights = grown / jnp.sum(grown, -1, keepdims=True)
        WA[h] = weights
        context = mm(weights.astype(BF16), QB[:, QW + HS :])
        CTX[:, span] = context.astype(BF16)
        CTT[span, :] = context.T.astype(BF16)
    send(None, ("ctt", CTT, CTP, {"section": other}))
    send(is1, ("q1", WQ1, WQ1, {"section": 0}), ("o1", WO1, WO1, {"section": 0}))

    recv(is0, ("wo_R", wo_half(yo, 0)), ("wo_L", wo_half(yo, 1)))
    send(is0, ("wo_co", wo_rows(yo), wo_rows(yo), {"section": 1}))
    recv(is1, ("wo_c", wo_rows(y)), ("wo_cl", wo_rows(yl)), ("wo_cr", wo_rows(yr)), ("wo_co", wo_rows(yo)))
    send(is1, ("ayr", a_item(y), a_item(y), {"dp": at_yr}), ("ayl", a_item(y), a_item(y), {"dp": at_yl}),
         ("ac", a_item(y), a_item(y), {"section": 0}))

    for c in range(2):
        @pl.loop(RING * c, RING * (c + 1))
        def _(t):
            span = pl.ds(pl.multiple_of(t * 512, 512), 512)
            OP[:, span] = mm(CTX[...], WO[:, span]).astype(BF16)

        side_cols = pl.ds(c * HALF, HALF)
        send(None, (f"o1r{c}", half_rows(OP, zo, 0).at[:, side_cols], FWD.at[0, :, side_cols], {"dp": at_zr}),
             (f"o1l{c}", half_rows(OP, zo, 1).at[:, side_cols], FWD.at[1, :, side_cols], {"dp": at_zl}))
    for c in range(2):
        side_cols = pl.ds(c * HALF, HALF)
        for side, tag, dest, at in ((0, "o1r", zr, at_zr), (1, "o1l", zl, at_zl)):
            recv(None, (f"{tag}{c}", FWD.at[side, :, side_cols]))

            @pl.loop(0, 2)
            def _(g):
                rows = pl.ds(pl.multiple_of(dest * SEQ + side * 32 + g * 16, 16), 16)
                part = pl.ds(pl.multiple_of(g * 16, 16), 16)
                OP[rows, side_cols] = (
                    OP[rows, side_cols].astype(F32) + FWD[side, part, side_cols].astype(F32)
                ).astype(BF16)

            send(None, (f"o2{side}{c}", OP.at[my_rows(dest), side_cols], LAND.at[side, :, side_cols], {"dp": at}))

    a_two = lambda yy, half: WKV1.at[yy, pl.ds(2 * half, 2), LO]
    recv(is1, ("bzR", b_two(zo, 0)), ("bzL", b_two(zo, 1)))
    send(is1, ("bco", b_item(zo), b_item(zo), {"section": 0}))
    for tag, yy, fwd, half, at in (("r", yl, "R", 0, at_yr), ("l", yr, "L", 1, at_yl)):
        recv(is1, ("ay" + tag, a_item(yy)))
        send(is1, ("ay" + fwd, a_two(yy, half), a_two(yy, half), {"dp": at}),
             ("ac" + tag, a_item(yy), a_item(yy), {"section": 0}))

    recv(None, *[(f"o2{side}{c}", LAND.at[side, :, pl.ds(c * HALF, HALF)]) for c in range(2) for side in range(2)])

    length = jnp.where(is0, lens[0, 0], lens[0, 1])
    NL[...] = jnp.zeros_like(NL)
    HL[...] = jnp.zeros_like(HL)

    def last_rows(g):
        return lax.broadcasted_iota(jnp.int32, (16, D), 0) + g * 16 == length - 1

    @pl.loop(0, 4)
    def _(g):
        part = pl.ds(pl.multiple_of(g * 16, 16), 16)
        own = pl.ds(pl.multiple_of(z * SEQ + g * 16, 16), 16)
        total = X[part, :].astype(F32) + (
            OP[own, :].astype(F32) + LAND[0, part, :].astype(F32) + LAND[1, part, :].astype(F32)
        )
        hidden = total.astype(BF16)
        H1[part, :] = hidden
        rows = hidden.astype(F32)
        unit = rows * lax.rsqrt(jnp.mean(rows * rows, -1, keepdims=True) + EPS)
        normed = (unit * GA[1]).astype(BF16)
        N1[part, :] = normed
        last = last_rows(g)
        NL[...] += jnp.sum(jnp.where(last, normed.astype(F32), 0.0), 0, keepdims=True)
        HL[...] += jnp.sum(jnp.where(last, rows, 0.0), 0, keepdims=True)

    for j in range(N_DP):
        S1[j] = NL[:, j * BLK : (j + 1) * BLK]
    exchange("e1", lambda peer, slot: S1.at[peer], R1)
    R1[N_DP - 1] = S1[dp]
    KVA1[...] = jnp.zeros_like(KVA1)

    def project1(yy):
        @pl.loop(0, RING)
        def _(zz):
            block = N1[:, pl.ds(pl.multiple_of((zz * RING + yy) * BLK, BLK), BLK)]
            KVA1[...] += mm(block, WKV1[yy, zz])

    recv(is0, ("q1", WQ1), ("o1", WO1), ("ac", a_item(y)),
         ("bc", b_item(z)), ("bcr", b_item(zl)), ("bcl", b_item(zr)), ("bco", b_item(zo)))
    project1(y)
    landed("e1", R1)
    for j in range(N_DP):
        X1[j : j + 1, :] = R1[j]
    back = mm(X1[...].astype(BF16), WQ1[...])
    for j in range(N_DP):
        T2[j] = back[j : j + 1, :]
    exchange("e2", lambda peer, slot: T2.at[slot], R2)
    R2[N_DP - 1] = T2[N_DP - 1]
    for tag, yy in (("r", yl), ("l", yr)):
        recv(is0, ("ac" + tag, a_item(yy)))
        project1(yy)
    recv(is1, ("ayR", a_two(yo, 0)), ("ayL", a_two(yo, 1)))
    send(is1, ("aco", a_item(yo), a_item(yo), {"section": 0}))
    recv(is0, ("aco", a_item(yo)))
    project1(yo)
    for g in range(RING):
        KC[g * SEQ : (g + 1) * SEQ, :] = KVA1[:, g * HS : (g + 1) * HS].astype(BF16)
        VC[g * SEQ : (g + 1) * SEQ, :] = KVA1[:, (RING + g) * HS : (RING + g + 1) * HS].astype(BF16)
    landed("e2", R2)
    q_row = R2[0]
    for j in range(1, N_DP):
        q_row = q_row + R2[j]
    for h in range(HEADS):
        Q16[h : h + 1, :] = q_row[:, h * HS : (h + 1) * HS]
    q_last = Q16[...].astype(BF16)

    h_i = lax.broadcasted_iota(jnp.int32, (HEADS, RING * SEQ), 0)
    k_i = lax.broadcasted_iota(jnp.int32, (HEADS, RING * SEQ), 1)
    seen1 = jnp.logical_and(h_i // GROUP == k_i // SEQ, k_i % SEQ < length)
    logits = nt(q_last, KC[...]) * SCALE
    grown = jnp.where(seen1, jnp.exp(jnp.where(seen1, logits, 0.0)), 0.0)
    weights1 = grown / jnp.sum(grown, -1, keepdims=True)
    probs1 = weights1.astype(BF16)
    context1 = mm(probs1, VC[...]).astype(BF16).astype(F32)
    for h in range(HEADS):
        S3[h] = context1[h : h + 1, :]
    exchange("e3", lambda peer, slot: S3.at[peer], R3)
    R3[N_DP - 1] = S3[dp]
    landed("e3", R3)
    for j in range(N_DP):
        X3[j : j + 1, :] = R3[j]
    x3 = X3[...].astype(BF16)
    for t in range(4):
        back = mm(x3, WO1[:, t * 1024 : (t + 1) * 1024])
        for j in range(N_DP):
            T4[j, :, t * 1024 : (t + 1) * 1024] = back[j : j + 1, :]
    exchange("e4", lambda peer, slot: T4.at[slot], R4)
    R4[N_DP - 1] = T4[N_DP - 1]
    landed("e4", R4)
    update = R4[0]
    for j in range(1, N_DP):
        update = update + R4[j]
    final = (HL[...] + update).astype(BF16).astype(F32)

    scale1 = lax.rsqrt(jnp.mean(final * final, -1, keepdims=True) + EPS)
    unit1 = final * scale1
    weighed = unit1 * HD[...]
    score = jnp.sum(weighed, -1, keepdims=True)
    mine_sc = m * 2 + s
    SCB[mine_sc] = jnp.broadcast_to(score, (1, HS))
    send(None, *[
        (f"sc{dm}{ds}", SCB.at[mine_sc], SCB.at[mine_sc], {"member": (m + dm) % 4, "section": (s + ds) % 2})
        for dm in range(4) for ds in range(2) if dm or ds
    ])
    toward = scale1 * (HD[...] - unit1 * (score / D))
    S6[...] = toward.astype(BF16).astype(F32)
    exchange("e6", lambda peer, slot: S6, R6)
    R6[N_DP - 1] = S6[...]
    recv(None, *[
        (f"sc{dm}{ds}", SCB.at[((m + 4 - dm) % 4) * 2 + (s + ds) % 2])
        for dm in range(4) for ds in range(2) if dm or ds
    ])
    chosen = (SCB[0] + SCB[2] + SCB[4] + SCB[6]) / 4
    rejected = (SCB[1] + SCB[3] + SCB[5] + SCB[7]) / 4
    spread = jax.nn.sigmoid(rejected - chosen)
    direction = jnp.where(is0, -spread, spread)
    landed("e6", R6)
    for j in range(N_DP):
        X6[j : j + 1, :] = R6[j]
    back = jnp.zeros((N_DP, HS), F32)
    for t in range(4):
        span = slice(t * 1024, (t + 1) * 1024)
        back = back + nt(X6[:, span].astype(BF16), WO1[:, span])
    for j in range(N_DP):
        T7[j] = back[j : j + 1, :]
    exchange("e7", lambda peer, slot: T7.at[slot], R7)
    R7[N_DP - 1] = T7[N_DP - 1]
    landed("e7", R7)
    for h in range(HEADS):
        DC[h : h + 1, :] = R7[slot_of(h)]
    d_ctx = (DC[...] * direction).astype(BF16)
    d_probs = nt(d_ctx, VC[...])
    leaned = weights1 * d_probs
    d_logits = (leaned - weights1 * jnp.sum(leaned, -1, keepdims=True)) * SCALE
    d_logits = d_logits.astype(BF16)
    d_query = mm(d_logits, KC[...]).astype(BF16).astype(F32)
    for h in range(HEADS):
        S8[:, h * HS : (h + 1) * HS] = d_query[h : h + 1, :]
    lane = lax.broadcasted_iota(jnp.int32, (1, HS), 1)
    meta = jnp.where(lane == 0, direction, jnp.where(lane == 1, chosen, rejected))
    S8[:, HEADS * HS :] = jnp.where(lane == 3, route[0].astype(F32), meta)
    exchange("e8", lambda peer, slot: S8, R8)
    R8[N_DP - 1] = S8[...]
    d_key = tn(d_logits, q_last)
    d_value = tn(probs1, d_ctx)
    for g in range(RING):
        DKV[:, g * HS : (g + 1) * HS] = d_key[g * SEQ : (g + 1) * SEQ, :].astype(BF16)
        DKV[:, (RING + g) * HS : (RING + g + 1) * HS] = d_value[g * SEQ : (g + 1) * SEQ, :].astype(BF16)

    @pl.loop(0, N_DP)
    def _(j):
        span = pl.ds(pl.multiple_of(j * BLK, BLK), BLK)
        GN[:, span] = nt(DKV[...], WKV1[j % RING, j // RING])

    landed("e8", R8)
    for j in range(N_DP):
        X8[j : j + 1, :] = R8[j, :, : HEADS * HS]
    back = nt(X8[...].astype(BF16), WQ1[...])
    for j in range(N_DP):
        T9[j] = back[j : j + 1, :]
    exchange("e9", lambda peer, slot: T9.at[slot], R9)
    R9[N_DP - 1] = T9[N_DP - 1]
    answer = jnp.zeros((1, HS), F32)
    for j in range(N_DP):
        extra = R8[j, :, HEADS * HS :]
        answer = answer + jnp.where(extra[:, 3:4] == dp.astype(F32), extra, 0.0)
        GC[s, j : j + 1, :] = R6[j] * extra[:, 0:1]
    scores_out[...] = answer[:, 1:3]
    XC[s] = X3[...]
    send(is0, ("xc", XC.at[0], XC.at[0], {"section": 1}), ("gc", GC.at[0], GC.at[0], {"section": 1}))
    landed("e9", R9)
    for h in range(N_DP):
        GNL[:, h * BLK : (h + 1) * BLK] = R9[slot_of(h)]

    HL[...] = (toward * direction[:, 0:1]).astype(BF16).astype(F32)
    NL[...] = jnp.zeros_like(NL)

    @pl.loop(0, 4)
    def _(g):
        part = pl.ds(pl.multiple_of(g * 16, 16), 16)
        rows = H1[part, :].astype(F32)
        scale = lax.rsqrt(jnp.mean(rows * rows, -1, keepdims=True) + EPS)
        unit = rows * scale
        last = last_rows(g)
        d_normed = GN[part, :] + jnp.where(last, GNL[...], 0.0)
        NL[...] += jnp.sum(d_normed * unit, 0, keepdims=True)
        pulled = d_normed * GA[1]
        d_rows = scale * (pulled - unit * jnp.mean(pulled * unit, -1, keepdims=True))
        d_rows = (d_rows + jnp.where(last, HL[...], 0.0)).astype(BF16)
        own = pl.ds(pl.multiple_of(z * SEQ + g * 16, 16), 16)
        for c in range(2):
            for half in range(2):
                first = half * HALF + c * QUART
                G[c, own, half * QUART : (half + 1) * QUART] = d_rows[:, first : first + QUART]

    across = pl.ds(pl.multiple_of(other * QUART, QUART), QUART)

    def to_core(c, n, zz):
        send(None, (f"gp{c}{n}", G.at[c, my_rows(zz), across], GP.at[c, my_rows(zz)], {"section": other}))

    for c in range(2):
        ring_z1(f"g{c}", G.at[c])
    for c in range(2):
        to_core(c, 0, z)

    recv(is1, ("xc", XC.at[0]), ("gc", GC.at[0]))

    @pl.when(is1)
    def _():
        rows_a, rows_b = XC[0].astype(BF16), XC[1].astype(BF16)

        @pl.loop(0, 8)
        def _(t):
            span = pl.ds(pl.multiple_of(t * 512, 512), 512)
            grad_out[0, 0, :, span] = (
                tn(rows_a, GC[0, :, span].astype(BF16)) + tn(rows_b, GC[1, :, span].astype(BF16))
            ).astype(BF16)

    for h in range(N_DP):
        SG[h, :, BLK:] = NL[:, h * BLK : (h + 1) * BLK]

    for c in range(2):
        ring_z2(f"g{c}", G.at[c])
        to_core(c, 1, zl)
        to_core(c, 2, zr)

    recv(None, ("ctt", CTP))

    def head_rows(c, yy):
        return GOP.at[c, pl.ds(pl.multiple_of(yy * HS, HS), HS)]

    def head_half(c, yy, half):
        return GOP.at[c, pl.ds(pl.multiple_of(yy * HS + half * 64, 64), 64)]

    def scatter1(c):
        ring_z3(f"g{c}", G.at[c])
        to_core(c, 3, zo)
        recv(None, *[(f"gp{c}{n}", GP.at[c, my_rows(zz)]) for n, zz in enumerate((z, zl, zr, zo))])

        @pl.loop(0, 2)
        def _(u):
            span = pl.ds(pl.multiple_of(u * 512, 512), 512)
            here = pl.ds(pl.multiple_of(s * QUART + u * 512, 512), 512)
            GOP[c, :, span] = (mm(CTT[...], G[c, :, here]) + mm(CTP[...], GP[c, :, span])).astype(BF16)

        send(None, (f"r1r{c}", head_half(c, yo, 0), FWD2.at[c, 0], {"dp": at_yr}),
             (f"r1l{c}", head_half(c, yo, 1), FWD2.at[c, 1], {"dp": at_yl}))
        send(is1, (f"rc{c}", head_rows(c, y), LAND2.at[c, 4], {"section": 0}))

    def scatter2(c):
        for side, tag, dest, at in ((0, "r1r", yr, at_yr), (1, "r1l", yl, at_yl)):
            recv(None, (f"{tag}{c}", FWD2.at[c, side]))
            rows = pl.ds(pl.multiple_of(dest * HS + side * 64, 64), 64)
            GOP[c, rows, :] = (GOP[c, rows, :].astype(F32) + FWD2[c, side].astype(F32)).astype(BF16)
            send(is0, (f"ra{side}{c}", head_rows(c, dest), LAND2.at[c, side], {"dp": at, "section": 0}))
            send(is1, (f"rb{side}{c}", head_rows(c, dest), LAND2.at[c, 2 + side], {"dp": at, "section": 0}))

    scatter1(0)
    scatter1(1)
    scatter2(0)

    DCT[...] = jnp.zeros_like(DCT)

    @pl.loop(0, 8)
    def _(t):
        c, u = t // RING, t % RING
        span = pl.ds(pl.multiple_of(u * 512, 512), 512)
        here = pl.ds(pl.multiple_of((u // 2) * HALF + c * QUART + (u % 2) * 512, 512), 512)
        DCT[...] += nt(G[c, :, span], WO[:, here])

    scatter2(1)

    d_key = jnp.zeros((ROWS, HS), F32)
    d_value = jnp.zeros((ROWS, HS), F32)
    for h in range(GROUP):
        span = slice(h * HS, (h + 1) * HS)
        d_ctx = DCT[:, span].astype(BF16)
        weights = WA[h]
        leaned = weights * nt(d_ctx, QB[:, QW + HS :])
        d_logits = (leaned - weights * jnp.sum(leaned, -1, keepdims=True)) * SCALE
        d_logits = d_logits.astype(BF16)
        DQB[:, span] = mm(d_logits, QB[:, QW : QW + HS]).astype(BF16)
        d_key = d_key + tn(d_logits, QB[:, span])
        d_value = d_value + tn(weights.astype(BF16), d_ctx)
    DQB[:, QW : QW + HS] = d_key.astype(BF16)
    DQB[:, QW + HS :] = d_value.astype(BF16)

    @pl.loop(0, N_DP)
    def _(j):
        span = pl.ds(pl.multiple_of(j * BLK, BLK), BLK)
        yy, zz = j % RING, j // RING
        d_normed = nt(DQB[...], W[yy, zz])
        sums = jnp.sum(d_normed * N[:, span].astype(F32), 0, keepdims=True)
        SG[j, :, :BLK] = sums / GA[0, :, span]

    exchange("e10", lambda peer, slot: SG.at[peer], RG)
    RG[N_DP - 1] = SG[dp]
    landed("e10", RG)
    total = RG[0]
    for j in range(1, N_DP):
        total = total + RG[j]
    SP[...] = total
    send(None, ("sp", SP, PG, {"section": other}))

    recv(None, ("sp", PG))
    both = total + PG[...]
    gain_out[0] = jnp.where(is0, both[:, :BLK], both[:, BLK:])

    for c in range(2):
        recv(is0, (f"rc{c}", LAND2.at[c, 4]), *[
            (f"r{kind}{side}{c}", LAND2.at[c, 2 * n + side]) for n, kind in enumerate("ab") for side in range(2)
        ])

    @pl.when(is0)
    def _():
        @pl.loop(0, 8)
        def _(g):
            part = pl.ds(pl.multiple_of(g * 16, 16), 16)
            own = pl.ds(pl.multiple_of(y * HS + g * 16, 16), 16)
            for c in range(2):
                grad_out[0, 0, part, c * QUART : (c + 1) * QUART] = (GOP[c, own, :].astype(F32) + (
                    LAND2[c, 0, part, :].astype(F32) + LAND2[c, 1, part, :].astype(F32)
                )).astype(BF16)
                grad_out[0, 0, part, HALF + c * QUART : HALF + (c + 1) * QUART] = (LAND2[c, 4, part, :].astype(F32) + (
                    LAND2[c, 2, part, :].astype(F32) + LAND2[c, 3, part, :].astype(F32)
                )).astype(BF16)

    for cond, fin in pending:
        guarded(cond, fin)
    assert len(ids) <= N_SEMS, len(ids)


def body(embeds, lengths, route, w_query, w_keyval, w_out, norm_gain, head):
    hbm = pl.BlockSpec(memory_space=pl.ANY)
    vmem = pl.BlockSpec(memory_space=pltpu.VMEM)
    smem = pl.BlockSpec(memory_space=pltpu.SMEM)
    V = pltpu.VMEM
    row = lambda n: V((1, n), F32)
    slots = lambda n: V((N_DP, 1, n), F32)
    scratch = [
        V((SEQ, D), BF16), V((2, 1, D), F32), row(D), V((ROWS, D), BF16),
        V((RING, RING, BLK, QW + 2 * HS), BF16), V((QW, D), BF16),
        V((BLK, HEADS * HS), BF16), V((HS, D), BF16), V((RING, RING, BLK, 2 * RING * HS), BF16),
        V((ROWS, QW + 2 * HS), F32), V((ROWS, QW + 2 * HS), BF16),
        V((GROUP, ROWS, ROWS), F32), V((ROWS, QW), BF16), V((QW, ROWS), BF16), V((QW, ROWS), BF16),
        V((ROWS, D), BF16), V((2, 32, D), BF16), V((2, SEQ, D), BF16),
        V((SEQ, D), BF16), V((SEQ, D), BF16), V((SEQ, 2 * RING * HS), F32),
        V((RING * SEQ, HS), BF16), V((RING * SEQ, HS), BF16), V((HEADS, HS), F32),
        row(D), row(D), slots(BLK), slots(BLK), V((N_DP, BLK), F32), slots(HEADS * HS), slots(HEADS * HS),
        slots(HS), slots(HS), V((N_DP, HS), F32), slots(D), slots(D), V((8, 1, HS), F32),
        row(D), slots(D), V((N_DP, D), F32), slots(HS), slots(HS), V((HEADS, HS), F32),
        row(HEADS * HS + HS), slots(HEADS * HS + HS), V((N_DP, HEADS * HS), F32), slots(BLK), slots(BLK),
        row(D), V((2, N_DP, HS), F32), V((2, N_DP, D), F32), V((SEQ, D), F32), V((SEQ, 2 * RING * HS), BF16),
        V((2, ROWS, HALF), BF16), V((2, ROWS, QUART), BF16), V((ROWS, QW), F32), V((ROWS, QW + 2 * HS), BF16),
        V((2, QW, QUART), BF16), V((2, 2, 64, QUART), BF16), V((2, 5, HS, QUART), BF16),
        slots(2 * BLK), slots(2 * BLK), row(2 * BLK), row(2 * BLK),
        pltpu.SemaphoreType.DMA((N_SEMS,)), pltpu.SemaphoreType.DMA((N_SEMS,)), pltpu.SemaphoreType.DMA((8,)),
    ]
    scores, grad, gains = pl.pallas_call(
        kernel,
        out_shape=(
            jax.ShapeDtypeStruct((1, 2), F32),
            jax.ShapeDtypeStruct((1, 1, HS, D), BF16),
            jax.ShapeDtypeStruct((1, 1, BLK), F32),
        ),
        in_specs=[hbm, smem, smem, hbm, hbm, hbm, hbm, hbm],
        out_specs=(vmem, vmem, vmem),
        scratch_shapes=scratch,
        compiler_params=pltpu.CompilerParams(
            collective_id=0, has_side_effects=True, vmem_limit_bytes=60 * 1024 * 1024
        ),
    )(embeds, lengths, route, w_query, w_keyval, w_out, norm_gain, head)
    return scores, grad.astype(F32), gains


def solution(mesh):
    placed = (
        P("member", "dp", None, None, None),
        P("dp", None),
        P("dp"),
        P("member", "section", "dp", None),
        P("member", "section", "dp", None),
        P("member", "section", "dp", None),
        P("member", "section", None),
        P("member", None),
    )
    return jax.shard_map(
        body,
        mesh=mesh,
        in_specs=placed,
        out_specs=(P("dp", None), P("member", "section", "dp", None), P("member", "section", "dp")),
        check_vma=False,
    )
```
